128 devices in a mesh: space: 16 (over x, z_lo, core), instance: 4 (over y), coarse: 2 (over z_hi).
Axes of the slice: x: 4, y: 4, z: 4 (z_hi: 2, z_lo: 2; z = z_hi * 2 + z_lo), core: 2. Of those that a mesh axis runs over, the one named last changes fastest.
Arguments:
- forcing: float32 [8, 5, 128, 32, 512], P('instance', None, 'space', 'coarse'), may hold values from -6 to 6
- state_start: float32 [8, 5, 128, 32, 512], P('instance', None, 'space', 'coarse'), may hold values from -6 to 6
- kappa: float32 [128, 32, 512], P('space', 'coarse'), may hold values from 0.25 to 4
- coupling: float32 [5, 5], replicated, may hold values from -1.25 to 1.25
- lag: int32 [32], P('coarse'), may hold values from 0 to 7
Outputs:
- state: float32 [8, 5, 128, 32, 512], P('instance', None, 'space', 'coarse')
The draws below stay inside these ranges and needn't reach their ends.
All inputs are finite; a program needn't handle non-finite values.
Results may differ from the reference program's by a relative error of at most 0.0001.
Values sent between devices are 32-bit elements; how exact they have to be, the bound alone decides.
A program may use at most 192 MiB of HBM per device.

```python
import math
import jax
import jax.numpy as jnp
from jax import lax

C = 5
INST = 8
FINE_CYCLES = 2
COARSE_SWEEPS = 2
NX = 128
NY = 512
NZ = 32


def place_ends(entries, own_key, low, top_value):
    extent = entries.shape
    spot = [jax.random.randint(jax.random.fold_in(own_key, axis), (), 0, extent[axis]) for axis in range(len(extent))]
    entries = entries.at[tuple(spot)].set(low)
    longest = extent.index(max(extent))
    spot[longest] = (spot[longest] + 1) % extent[longest]
    return entries.at[tuple(spot)].set(top_value)


def steps_of(own_key, dims, shards, smallest, largest):
    loudness, own = 1.0, jax.random.fold_in(own_key, 6)
    for axis_at, blocks in shards:
        draws = jnp.exp(jax.random.uniform(jax.random.fold_in(own, axis_at), (blocks,), jnp.float32, smallest / len(shards), largest / len(shards)))
        loudness = loudness * jnp.repeat(draws, dims[axis_at] // blocks).reshape([-1 if axis == axis_at else 1 for axis in range(len(dims))])
    return loudness


def scatter_about(rng, shape, deviation, reach, split=(), held_as=jnp.bfloat16):
    drawn = jax.random.normal(rng, shape, jnp.float32) * deviation
    if len(split) > 0:
        drawn = steps_of(rng, shape, split, -0.22, 0.18) * drawn
    return jnp.clip(drawn, min=-reach, max=reach).astype(held_as)


def setup_inputs(seed: int = 0) -> dict:
    key_of = jax.random.split(jax.random.key(seed), 6)
    forcing = scatter_about(key_of[0], (INST, C, NX, NZ, NY), 1.0, 6.0, ((0, 4), (2, 16), (3, 2)), jnp.float32)
    state_start = scatter_about(key_of[1], (INST, C, NX, NZ, NY), 1.0, 6.0, ((0, 4), (2, 16), (3, 2)), jnp.float32)
    kappa = jnp.clip(jnp.exp(math.log(4.0) - 2.7725887 * jax.random.uniform(key_of[2], (NX, NZ, NY), jnp.float32) ** steps_of(key_of[2], (NX, NZ, NY), ((0, 16), (1, 2)), -0.2, 0.2)), 0.25, 4.0)
    coupling = scatter_about(key_of[3], (C, C), 20 ** -0.5, 1.25, (), jnp.float32)
    lag = place_ends(jax.random.randint(key_of[4], (NZ,), 0, INST), jax.random.fold_in(key_of[4], 1), 0, INST - 1).astype(jnp.int32)
    return dict(forcing=forcing, state_start=state_start, kappa=kappa, coupling=coupling, lag=lag)


HIGH = lax.Precision.HIGHEST


def spectral_matrix(count):
    diff = jnp.arange(count, dtype=jnp.int32)[:, None] - jnp.arange(count, dtype=jnp.int32)[None, :]
    sign = (1 - 2 * (jnp.abs(diff) % 2)).astype(jnp.float32)
    angle = jnp.pi * diff.astype(jnp.float32) / count
    sine = jnp.where(diff == 0, jnp.float32(1.0), jnp.sin(angle))
    return jnp.where(diff == 0, jnp.float32(0.0), 0.5 * sign * jnp.cos(angle) / sine)


def residual_of(field, source, low_ghost, high_ghost, forcing, kappa, coupling):
    padded = jnp.pad(field, ((0, 0), (0, 0), (1, 1), (1, 1), (0, 0)))
    beside = padded[:, :, 2:, 1:-1] + padded[:, :, :-2, 1:-1]
    beside = beside + padded[:, :, 1:-1, 2:] + padded[:, :, 1:-1, :-2]
    length = field.shape[4]
    column = jnp.arange(length, dtype=jnp.int32)
    upper = jnp.where(column == length - 1, high_ghost[..., None], jnp.roll(field, -1, axis=4))
    lower = jnp.where(column == 0, low_ghost[..., None], jnp.roll(field, 1, axis=4))
    mixed = jnp.einsum("cd,ndxzy->ncxzy", coupling, field, precision=HIGH)
    return forcing - source - (6.0 + kappa) * field + beside + upper + lower - mixed


def coarse_apply(field, padded, kappa_c, coupling):
    beside = padded[:, :, 2:, 1:-1] + padded[:, :, :-2, 1:-1]
    beside = beside + padded[:, :, 1:-1, 2:] + padded[:, :, 1:-1, :-2]
    beside = beside + jnp.roll(field, 1, axis=4) + jnp.roll(field, -1, axis=4)
    mixed = jnp.einsum("cd,ndxzy->ncxzy", coupling, field, precision=HIGH)
    return (6.0 + kappa_c) * field - beside + mixed


def reference(forcing, state_start, kappa, coupling, lag):
    spectral = spectral_matrix(INST)
    source = jnp.einsum("nk,kcxzy->ncxzy", spectral, state_start, precision=HIGH)
    slots = jnp.arange(INST, dtype=jnp.int32)
    low_idx = (slots[:, None] - lag[None, :]) % INST
    high_idx = (slots[:, None] + lag[None, :]) % INST
    low_pick = (low_idx[:, None, :] == slots[None, :, None]).astype(jnp.float32)
    high_pick = (high_idx[:, None, :] == slots[None, :, None]).astype(jnp.float32)
    low_ghost = jnp.einsum("nkz,kcxz->ncxz", low_pick, state_start[:, :, :, :, NY - 1], precision=HIGH)
    high_ghost = jnp.einsum("nkz,kcxz->ncxz", high_pick, state_start[:, :, :, :, 0], precision=HIGH)
    step = 0.8 / (6.0 + kappa)
    field = state_start
    for cycle in range(FINE_CYCLES):
        begin = field
        for weight in (0.25, 0.5, 1.0):
            field = begin + weight * step * residual_of(field, source, low_ghost, high_ghost, forcing, kappa, coupling)
    last = residual_of(field, source, low_ghost, high_ghost, forcing, kappa, coupling)
    rhs_c = last.reshape(INST, C, NX // 2, 2, NZ // 2, 2, NY // 2, 2).sum(axis=(3, 5, 7))
    kappa_c = kappa.reshape(NX // 2, 2, NZ // 2, 2, NY // 2, 2).mean(axis=(1, 3, 5))
    corr = jnp.zeros_like(rhs_c)
    for sweep in range(COARSE_SWEEPS):
        padded = jnp.pad(corr, ((0, 0), (0, 0), (1, 1), (1, 1), (0, 0)))
        corr = corr + 0.8 / (6.0 + kappa_c) * (rhs_c - coarse_apply(corr, padded, kappa_c, coupling))
    fine_corr = jnp.broadcast_to(corr[:, :, :, None, :, None, :, None], (INST, C, NX // 2, 2, NZ // 2, 2, NY // 2, 2))
    return field + fine_corr.reshape(INST, C, NX, NZ, NY)
```

```python
import functools
import math

import jax
import jax.numpy as jnp
import numpy as np
from jax import lax
from jax.experimental import pallas as pl
from jax.experimental.pallas import tpu as pltpu
from jax.sharding import PartitionSpec as P

MESH = pl.DeviceIdType.MESH
WEIGHTS = (0.25, 0.5, 1.0)
STAGES = 6
NEAR = 12
LOOKAHEAD = 2


def spectral(d):
    if d == 0:
        return 0.0
    return float(0.5 * (-1.0) ** abs(d) * math.cos(math.pi * d / 8) / math.sin(math.pi * d / 8))


D1, D2, D3, D4 = spectral(1), spectral(2), spectral(3), spectral(4)


def leg_kernel(
    forcing, start, kappa, coupling, lag, out_u, out_e,
    S, A, B, F, R1, C2, R2, K, W, E, EG, GP, RHS, WC, E1, E2,
    ld_s, ld_f, ld_k, p1s, p1r, p2s, p2r, es, er, xs_s, xs_r, zs_s, zs_r, cx_s, cx_r, cz_s, cz_r, out_sem,
):
    comps = 5
    sp, it, co = lax.axis_index("space"), lax.axis_index("instance"), lax.axis_index("coarse")
    spaces = lax.axis_size("space")
    odd = lax.rem(it, 2)
    pa = lax.rem(it + 1 + 2 * odd, 4)
    pb = lax.rem(it + 3 + 2 * odd, 4)
    has_lo, has_hi = sp > 0, sp < spaces - 1

    sub = lax.broadcasted_iota(jnp.int32, (8, 128), 0)
    lane = lax.broadcasted_iota(jnp.int32, (8, 128), 1)
    inst = sub // 4
    quarter = sub % 4

    sign = 2 * co - 1
    base = 15 * (1 - co)

    def zcell(d):
        return base + sign * d

    def zrange(d0, d1):
        return (1 - co) * (16 - d1) + co * d0

    order = (0, 7, 1, 6, 2, 5, 3, 4)
    for x in order:
        for n in range(2):
            for q in range(4):
                pltpu.make_async_copy(
                    start.at[n, :, x, :, pl.ds(q * 128, 128)],
                    S.at[x + 1, :, pl.ds(1, 16), n * 4 + q, :], ld_s.at[x],
                ).start()
    for n in range(2):
        for q in range(4):
            pltpu.make_async_copy(
                kappa.at[:, :, pl.ds(q * 128, 128)], K.at[:, :, n * 4 + q, :], ld_k.at[0]
            ).start()
    for x in order:
        for n in range(2):
            for q in range(4):
                pltpu.make_async_copy(
                    forcing.at[n, :, x, :, pl.ds(q * 128, 128)],
                    F.at[x, :, :, n * 4 + q, :], ld_f.at[x],
                ).start()

    zero16 = jnp.zeros((comps, 16, 8, 128), jnp.float32)
    zero1 = jnp.zeros((comps, 8, 128), jnp.float32)
    zero8 = jnp.zeros((comps, 8, 8, 128), jnp.float32)
    zend = 17 * co
    zend_c = 9 * co

    for x in range(8):
        for buf in (S, A, B):
            buf[x + 1, :, zend] = zero1
    for x in range(4):
        E1[x + 1, :, zend_c] = zero1

    @pl.when(sp == 0)
    def _():
        for buf in (S, A, B):
            buf[0, :, pl.ds(1, 16)] = zero16
        E1[0, :, pl.ds(1, 8)] = zero8

    @pl.when(sp == spaces - 1)
    def _():
        for buf in (S, A, B):
            buf[9, :, pl.ds(1, 16)] = zero16
        E1[5, :, pl.ds(1, 8)] = zero8

    bar = pltpu.get_barrier_semaphore()
    for r in (1, 2, 3):
        pl.semaphore_signal(bar, inc=1, device_id={"instance": lax.rem(it + r, 4)}, device_id_type=MESH)
    pl.semaphore_signal(bar, inc=1, device_id={"coarse": 1 - co}, device_id_type=MESH)

    @pl.when(has_lo)
    def _():
        pl.semaphore_signal(bar, inc=1, device_id={"space": sp - 1}, device_id_type=MESH)

    @pl.when(has_hi)
    def _():
        pl.semaphore_signal(bar, inc=1, device_id={"space": sp + 1}, device_id_type=MESH)

    pl.semaphore_wait(bar, 4 + has_lo.astype(jnp.int32) + has_hi.astype(jnp.int32))

    halves = ((0, NEAR), (NEAR, 16))

    def level_buf(level):
        return (S, A, B)[level % 3]

    def level_range(level, h):
        cut = NEAR - max(level - 1, 0)
        return (0, cut) if h == 0 else (cut, 16)

    def xface(level, h, side):
        buf = level_buf(level)
        d0, d1 = level_range(level, h)
        z0 = 1 + zrange(d0, d1)
        i = ((level % 3) * 2 + h) * 2 + side
        src = buf.at[1 if side == 0 else 8, :, pl.ds(z0, d1 - d0)]
        dst = buf.at[9 if side == 0 else 0, :, pl.ds(z0, d1 - d0)]
        return pltpu.make_async_remote_copy(
            src, dst, xs_s.at[i], xs_r.at[i],
            device_id={"space": sp - 1 if side == 0 else sp + 1}, device_id_type=MESH,
        )

    def x_send(level, h):
        pl.when(has_lo)(lambda: xface(level, h, 0).start())
        pl.when(has_hi)(lambda: xface(level, h, 1).start())

    def x_sent(level, h):
        pl.when(has_lo)(lambda: xface(level, h, 0).wait_send())
        pl.when(has_hi)(lambda: xface(level, h, 1).wait_send())

    def x_recv(level, h):
        pl.when(has_hi)(lambda: xface(level, h, 0).wait_recv())
        pl.when(has_lo)(lambda: xface(level, h, 1).wait_recv())

    def zface(level, x):
        buf = level_buf(level)
        i = (level % 3) * 8 + x
        return pltpu.make_async_remote_copy(
            buf.at[x + 1, :, pl.ds(1 + base, 1)], buf.at[x + 1, :, pl.ds(17 * co_other(), 1)],
            zs_s.at[i], zs_r.at[i], device_id={"coarse": 1 - co}, device_id_type=MESH,
        )

    def co_other():
        return co

    def raw(q, x, partner):
        h, t = divmod(q, 4)
        d0, d1 = halves[h]
        z0 = zrange(d0, d1)
        i = q * 2 + (0 if x < 4 else 1)
        return pltpu.make_async_remote_copy(
            S.at[x + 1, :, pl.ds(1 + z0, d1 - d0)], R1.at[x, :, pl.ds(z0, d1 - d0)],
            p1s.at[i], p1r.at[i], device_id={"instance": partner}, device_id_type=MESH,
        )

    def sums(q, x, partner):
        h, t = divmod(q, 4)
        d0, d1 = halves[h]
        z0 = zrange(d0, d1)
        i = q * 2 + (0 if x < 4 else 1)
        return pltpu.make_async_remote_copy(
            C2.at[x, :, pl.ds(z0, d1 - d0)], R2.at[x, :, pl.ds(z0, d1 - d0)],
            p2s.at[i], p2r.at[i], device_id={"instance": partner}, device_id_type=MESH,
        )

    def planes(q):
        t = q % 4
        return ((t, pa, pb), (7 - t, pb, pa))

    def raw_start(q):
        for x, first, second in planes(q):
            raw(q, x, first).start()

    def wait_state(x):
        view = S.at[x + 1, :, pl.ds(1, 16)]
        pltpu.make_async_copy(view, view, ld_s.at[x]).wait()

    for x in order:
        wait_state(x)
        if x >= 4 and 7 - x < LOOKAHEAD:
            raw_start(7 - x)
    x_send(0, 0)
    x_send(0, 1)
    for x in order:
        zface(0, x).start()

    def pack(z, carry):
        for xh in range(2):
            for xq in range(4):
                spot = xq * 32 + 2 * z
                mine = (lane // 2) == xq * 16 + z
                for c in range(comps):
                    v = pltpu.roll(S[xh * 4 + xq + 1, c, z + 1], spot + 1, 1)
                    E[c, xh] = jnp.where(mine, v, E[c, xh])
        return carry

    E[...] = jnp.zeros_like(E)
    lax.fori_loop(0, 16, pack, 0)

    def edge(r):
        return pltpu.make_async_remote_copy(
            E, EG.at[r - 1], es.at[r - 1], er.at[r - 1],
            device_id={"instance": lax.rem(it + r, 4)}, device_id_type=MESH,
        )

    for r in (1, 2, 3):
        edge(r).start()

    pltpu.make_async_copy(K, K, ld_k.at[0]).wait()
    even_lane = lane % 2 == 0

    def pair_sum(v):
        return v + jnp.where(even_lane, pltpu.roll(v, 127, 1), pltpu.roll(v, 1, 1))

    def steps(zc, carry):
        for xc in range(4):
            total = None
            for dx in range(2):
                for dz in range(2):
                    k = K[2 * xc + dx, 2 * zc + dz]
                    W[2 * xc + dx, 2 * zc + dz] = 0.8 / (6.0 + k)
                    total = k if total is None else total + k
            WC[xc, zc] = 0.8 / (6.0 + pair_sum(total) * 0.125)
        return carry

    lax.fori_loop(0, 8, steps, 0)

    for x in order:
        view = F.at[x]
        pltpu.make_async_copy(view, view, ld_f.at[x]).wait()

    def ghosts():
        zl = (lane % 32) // 2
        lags = jnp.zeros((8, 128), jnp.int32)
        for z in range(16):
            lags = jnp.where(zl == z, lag[z], lags)
        mine = 2 * it + inst
        low = (mine - lags + 8) % 8
        high = (mine + lags) % 8
        want = jnp.where(
            (quarter == 0) & (lane % 2 == 1), low, jnp.where((quarter == 3) & (lane % 2 == 0), high, -1)
        )
        low_slot = lane % 2 == 1
        for r in (1, 2, 3):
            edge(r).wait_recv()
        for c in range(comps):
            for xh in range(2):
                total = jnp.zeros((8, 128), jnp.float32)
                for r in range(4):
                    p = E[c, xh] if r == 0 else EG[r - 1, c, xh]
                    who = lax.rem(it + 4 - r, 4)
                    up, down = pltpu.roll(p, 1, 1), pltpu.roll(p, 127, 1)
                    same = jnp.where(low_slot, pltpu.roll(up, 5, 0), pltpu.roll(down, 3, 0))
                    other = jnp.where(low_slot, pltpu.roll(up, 1, 0), pltpu.roll(down, 7, 0))
                    total = jnp.where(want == 2 * who + inst, same, total)
                    total = jnp.where(want == 2 * who + 1 - inst, other, total)
                GP[c, xh] = total

        ends = ((lane == 0) & (quarter == 0)) | ((lane == 127) & (quarter == 3))

        def unpack(z, carry):
            for xh in range(2):
                for xq in range(4):
                    back = 127 - xq * 32 - 2 * z
                    for c in range(comps):
                        v = pltpu.roll(GP[c, xh], back, 1)
                        x = xh * 4 + xq
                        F[x, c, z] = F[x, c, z] + jnp.where(ends, v, 0.0)
            return carry

        lax.fori_loop(0, 16, unpack, 0)

    def by_inst(v0, v1):
        return jnp.where(inst == 0, v0, v1).astype(jnp.float32)

    delta = by_inst(-D1, D1)
    gamma = by_inst(D3, -D3)
    plus = by_inst(D1, D3)
    minus = by_inst(-D3, -D1)

    def source_part(q):
        h, t = divmod(q, 4)
        d0, d1 = halves[h]
        z0 = zrange(d0, d1)
        for x, first, second in planes(q):
            raw(q, x, first).wait_recv()
        for x, first, second in planes(q):
            up = odd == (1 if x < 4 else 0)
            alpha = jnp.where(up, D2, -D2).astype(jnp.float32)
            beta = jnp.where(up, plus, minus)

            def part(i, carry):
                z = z0 + i
                for c in range(comps):
                    u, v = S[x + 1, c, z + 1], R1[x, c, z]
                    ur, vr = pltpu.roll(u, 4, 0), pltpu.roll(v, 4, 0)
                    C2[x, c, z] = alpha * u + beta * ur + D4 * v + gamma * vr
                    F[x, c, z] = F[x, c, z] - (delta * ur + alpha * v + beta * vr)
                return carry

            lax.fori_loop(0, d1 - d0, part, 0)
            sums(q, x, second).start()

    def source_rest(q):
        h, t = divmod(q, 4)
        d0, d1 = halves[h]
        z0 = zrange(d0, d1)
        for x, first, second in planes(q):
            sums(q, x, second).wait_recv()
            raw(q, x, first).wait_send()

        def rest(i, carry):
            z = z0 + i
            for x, first, second in planes(q):
                for c in range(comps):
                    F[x, c, z] = F[x, c, z] - R2[x, c, z]
            return carry

        lax.fori_loop(0, d1 - d0, rest, 0)

    lane_lo, lane_hi = lane == 0, lane == 127
    fix_lo = lane_lo & (quarter != 0)
    fix_hi = lane_hi & (quarter != 3)
    zero = jnp.zeros((8, 128), jnp.float32)

    def beside_y(u):
        lo, hi = pltpu.roll(u, 1, 1), pltpu.roll(u, 127, 1)
        lower = jnp.where(fix_lo, pltpu.roll(lo, 1, 0), jnp.where(lane_lo, zero, lo))
        upper = jnp.where(fix_hi, pltpu.roll(hi, 7, 0), jnp.where(lane_hi, zero, hi))
        return lower + upper

    def mix(us, c):
        total = coupling[c, 0] * us[0]
        for d in range(1, comps):
            total = total + coupling[c, d] * us[d]
        return total

    def balance(src, x, z, us):
        got = []
        for c in range(comps):
            near = (src[x, c, z + 1] + src[x + 2, c, z + 1]) + (src[x + 1, c, z] + src[x + 1, c, z + 2])
            got.append((F[x, c, z] + near) + (beside_y(us[c]) - mix(us, c)))
        return got

    def stage_block(k, j, h):
        src, dst = level_buf(k - 1), level_buf(k)
        d0, d1 = level_range(k, h)
        weight = WEIGHTS[(k - 1) % 3]
        begin = S

        def body(d, carry):
            z = zcell(d)
            for x in (j, 7 - j):
                us = [src[x + 1, c, z + 1] for c in range(comps)]
                bal = balance(src, x, z, us)
                w = W[x, z] * weight
                for c in range(comps):
                    own = us[c] if (k - 1) % 3 == 0 else begin[x + 1, c, z + 1]
                    dst[x + 1, c, z + 1] = (own - (0.8 * weight) * us[c]) + w * bal[c]
            return carry

        lax.fori_loop(d0, d1, body, 0)

    def last_block(j, h):
        d0, d1 = level_range(7, h)

        def body(m, carry):
            zc = (1 - co) * (7 - m) + co * m
            for x in (j, 7 - j):
                total = [None] * comps
                for dz in range(2):
                    z = 2 * zc + dz
                    us = [S[x + 1, c, z + 1] for c in range(comps)]
                    bal = balance(S, x, z, us)
                    diag = 6.0 + K[x, z]
                    for c in range(comps):
                        res = bal[c] - diag * us[c]
                        total[c] = res if total[c] is None else total[c] + res
                for c in range(comps):
                    if j % 2 == 0:
                        RHS[x // 2, c, zc] = total[c]
                    else:
                        RHS[x // 2, c, zc] = RHS[x // 2, c, zc] + total[c]
            return carry

        lax.fori_loop(d0 // 2, d1 // 2, body, 0)

    def run(k, j, h):
        if j == 0:
            x_recv(k - 1, h)
            if 3 <= k <= STAGES:
                x_sent(k - 3, h)
        if h == 0:
            for x in (j, 7 - j):
                zface(k - 1, x).wait_recv()
                if 3 <= k <= STAGES:
                    zface(k - 3, x).wait_send()
        if k <= STAGES:
            stage_block(k, j, h)
            if j == 0:
                x_send(k, h)
            if h == 0:
                for x in (j, 7 - j):
                    zface(k, x).start()
            if k == STAGES and h == 1:
                for x in (j, 7 - j):
                    u_out(x).start()
        else:
            last_block(j, h)

    def u_out(x):
        return pltpu.make_async_copy(S.at[x + 1, :, pl.ds(1, 16)], out_u.at[x], out_sem.at[x])

    def wave(t, h):
        for k in range(1, STAGES + 2):
            j = t - k + 1
            if 0 <= j <= 3:
                run(k, j, h)

    def first_sweep(xc):
        def body(zc, carry):
            for c in range(comps):
                E1[xc + 1, c, zc + 1] = WC[xc, zc] * pair_sum(RHS[xc, c, zc])
            return carry

        lax.fori_loop(0, 8, body, 0)

    def cx(side):
        return pltpu.make_async_remote_copy(
            E1.at[1 if side == 0 else 4, :, pl.ds(1, 8)], E1.at[5 if side == 0 else 0, :, pl.ds(1, 8)],
            cx_s.at[side], cx_r.at[side],
            device_id={"space": sp - 1 if side == 0 else sp + 1}, device_id_type=MESH,
        )

    def cz(xc):
        return pltpu.make_async_remote_copy(
            E1.at[xc + 1, :, pl.ds(1 + 7 * (1 - co), 1)], E1.at[xc + 1, :, pl.ds(9 * co, 1)],
            cz_s.at[xc], cz_r.at[xc], device_id={"coarse": 1 - co}, device_id_type=MESH,
        )

    lo2, hi2 = lane < 2, lane >= 126
    first_q, last_q = quarter == 0, quarter == 3

    def beside_y2(u):
        lo, hi = pltpu.roll(u, 2, 1), pltpu.roll(u, 126, 1)
        wrap_lo = jnp.where(first_q, pltpu.roll(lo, 5, 0), pltpu.roll(lo, 1, 0))
        wrap_hi = jnp.where(last_q, pltpu.roll(hi, 3, 0), pltpu.roll(hi, 7, 0))
        return jnp.where(lo2, wrap_lo, lo) + jnp.where(hi2, wrap_hi, hi)

    def second_sweep(xc):
        def body(zc, carry):
            es_ = [E1[xc + 1, c, zc + 1] for c in range(comps)]
            w = WC[xc, zc]
            for c in range(comps):
                near = (E1[xc, c, zc + 1] + E1[xc + 2, c, zc + 1]) + (E1[xc + 1, c, zc] + E1[xc + 1, c, zc + 2])
                E2[xc, c, zc] = 1.2 * es_[c] + w * ((near + beside_y2(es_[c])) - mix(es_, c))
            return carry

        lax.fori_loop(0, 8, body, 0)

    for q in range(8):
        source_part(q)
        if q + LOOKAHEAD < 8:
            raw_start(q + LOOKAHEAD)
        if q == 0:
            ghosts()
        if q >= 1:
            source_rest(q - 1)
            if q <= 4:
                wave(q - 1, 0)
            else:
                wave(q - 5, 1)
                if q == 6:
                    wave(4, 0)
    source_rest(7)
    wave(3, 1)
    wave(5, 0)
    wave(6, 0)
    wave(4, 1)
    wave(7, 0)
    wave(5, 1)
    wave(8, 0)
    wave(9, 0)
    wave(6, 1)
    wave(7, 1)
    first_sweep(0)
    first_sweep(3)
    pl.when(has_lo)(lambda: cx(0).start())
    pl.when(has_hi)(lambda: cx(1).start())
    cz(0).start()
    cz(3).start()
    wave(8, 1)
    wave(9, 1)
    first_sweep(1)
    first_sweep(2)
    cz(1).start()
    cz(2).start()
    for xc in (1, 2):
        cz(xc).wait_recv()
        second_sweep(xc)
    pl.when(has_hi)(lambda: cx(0).wait_recv())
    pl.when(has_lo)(lambda: cx(1).wait_recv())
    for xc in (0, 3):
        cz(xc).wait_recv()
        second_sweep(xc)
    final = pltpu.make_async_copy(E2, out_e, out_sem.at[8])
    final.start()

    for level in (4, 5, 6):
        for h in range(2):
            x_sent(level, h)
        for x in range(8):
            zface(level, x).wait_send()
    for q in range(8):
        for x, first, second in planes(q):
            sums(q, x, second).wait_send()
    for r in (1, 2, 3):
        edge(r).wait_send()
    pl.when(has_lo)(lambda: cx(0).wait_send())
    pl.when(has_hi)(lambda: cx(1).wait_send())
    for xc in range(4):
        cz(xc).wait_send()
    for x in range(8):
        u_out(x).wait()
    final.wait()


def leg(forcing, start, kappa, coupling, lag):
    f32 = jnp.float32
    vmem = pltpu.VMEM
    dma = pltpu.SemaphoreType.DMA
    hbm = pl.BlockSpec(memory_space=pltpu.HBM)
    smem = pl.BlockSpec(memory_space=pltpu.SMEM)
    halo = (10, 5, 18, 8, 128)
    block = (8, 5, 16, 8, 128)
    return pl.pallas_call(
        leg_kernel,
        out_shape=(jax.ShapeDtypeStruct(block, f32), jax.ShapeDtypeStruct((4, 5, 8, 8, 128), f32)),
        in_specs=[hbm, hbm, hbm, smem, smem],
        out_specs=(hbm, hbm),
        scratch_shapes=[
            vmem(halo, f32), vmem(halo, f32), vmem(halo, f32),
            vmem(block, f32), vmem(block, f32), vmem(block, f32), vmem(block, f32),
            vmem((8, 16, 8, 128), f32), vmem((8, 16, 8, 128), f32),
            vmem((5, 2, 8, 128), f32), vmem((3, 5, 2, 8, 128), f32), vmem((5, 2, 8, 128), f32),
            vmem((4, 5, 8, 8, 128), f32), vmem((4, 8, 8, 128), f32),
            vmem((6, 5, 10, 8, 128), f32), vmem((4, 5, 8, 8, 128), f32),
            dma((8,)), dma((8,)), dma((1,)),
            dma((16,)), dma((16,)), dma((16,)), dma((16,)),
            dma((3,)), dma((3,)),
            dma((12,)), dma((12,)), dma((24,)), dma((24,)),
            dma((2,)), dma((2,)), dma((4,)), dma((4,)), dma((9,)),
        ],
        compiler_params=pltpu.CompilerParams(
            collective_id=0, has_side_effects=True, vmem_limit_bytes=56 * 2**20
        ),
        name="leg",
    )(forcing, start, kappa, coupling, lag)


def add_kernel(u_ref, e_ref, o_ref):
    for c in range(5):
        e = e_ref[0, c]
        v = u_ref[0, c].reshape(8, 2, 8, 128) + e[:, None]
        v = jnp.swapaxes(v.reshape(16, 8, 128), 0, 1)
        for n in range(2):
            for q in range(4):
                o_ref[n, c, 0, :, q * 128 : (q + 1) * 128] = v[n * 4 + q]


def add_correction(u, e):
    return pl.pallas_call(
        add_kernel,
        grid=(8,),
        out_shape=jax.ShapeDtypeStruct((2, 5, 8, 16, 512), jnp.float32),
        in_specs=[
            pl.BlockSpec((1, 5, 16, 8, 128), lambda x: (x, 0, 0, 0, 0)),
            pl.BlockSpec((1, 5, 8, 8, 128), lambda x: (x // 2, 0, 0, 0, 0)),
        ],
        out_specs=pl.BlockSpec((2, 5, 1, 16, 512), lambda x: (0, 0, x, 0, 0)),
        compiler_params=pltpu.CompilerParams(vmem_limit_bytes=32 * 2**20),
        name="add_correction",
    )(u, e)


def shards(forcing, state_start, kappa, coupling, lag):
    u, e = leg(forcing, state_start, kappa, coupling, lag)
    return add_correction(u, e)


def solution(mesh):
    return jax.shard_map(
        shards,
        mesh=mesh,
        in_specs=(
            P("instance", None, "space", "coarse", None),
            P("instance", None, "space", "coarse", None),
            P("space", "coarse", None),
            P(),
            P("coarse"),
        ),
        out_specs=P("instance", None, "space", "coarse", None),
        check_vma=False,
    )
```

```python
import functools
import math

import jax
import jax.numpy as jnp
import numpy as np
from jax import lax
from jax.experimental import pallas as pl
from jax.experimental.pallas import tpu as pltpu
from jax.sharding import PartitionSpec as P

MESH = pl.DeviceIdType.MESH
WEIGHTS = (0.25, 0.5, 1.0)
STAGES = 6
CUTS = (0, 8, 12, 16)
SLABS = len(CUTS) - 1
CHUNKS = 4 * SLABS
LOOKAHEAD = 3
WIDE = 4


def spectral(d):
    if d == 0:
        return 0.0
    return float(0.5 * (-1.0) ** abs(d) * math.cos(math.pi * d / 8) / math.sin(math.pi * d / 8))


D1, D2, D3, D4 = spectral(1), spectral(2), spectral(3), spectral(4)


def leg_kernel(
    forcing, start, kappa, coupling, lag, out,
    S, A, B, F, R1, C2, R2, K, W, E, EG, GP, RHS, WC, E1, XO, XI, ZO, ZI,
    ld_s, ld_f, ld_k, p1s, p1r, p2s, p2r, es, er, xs_s, xs_r, zs_s, zs_r, px_s, px_r, pz_s, pz_r, out_sem,
):
    comps = 5
    sp, it, co = lax.axis_index("space"), lax.axis_index("instance"), lax.axis_index("coarse")
    spaces = lax.axis_size("space")
    odd = lax.rem(it, 2)
    pa = lax.rem(it + 1 + 2 * odd, 4)
    pb = lax.rem(it + 3 + 2 * odd, 4)
    has_lo, has_hi = sp > 0, sp < spaces - 1

    sub = lax.broadcasted_iota(jnp.int32, (8, 128), 0)
    lane = lax.broadcasted_iota(jnp.int32, (8, 128), 1)
    inst = sub // 4
    quarter = sub % 4

    def zrange(d0, d1):
        return (1 - co) * (16 - d1) + co * d0

    def turn(v, shift, axis):
        if v.ndim == 2:
            return pltpu.roll(v, shift, axis)
        if axis == 1:
            return pltpu.roll(v.reshape(-1, 128), shift, 1).reshape(v.shape)
        return jnp.stack([pltpu.roll(v[i], shift, 0) for i in range(v.shape[0])])

    order = (0, 7, 1, 6, 2, 5, 3, 4)
    for x in order:
        for n in range(2):
            for q in range(4):
                pltpu.make_async_copy(
                    start.at[n, :, x, :, pl.ds(q * 128, 128)],
                    S.at[x + 1, :, pl.ds(1, 16), n * 4 + q, :], ld_s.at[x],
                ).start()
    for n in range(2):
        for q in range(4):
            pltpu.make_async_copy(
                kappa.at[:, :, pl.ds(q * 128, 128)], K.at[:, :, n * 4 + q, :], ld_k.at[0]
            ).start()
    for x in order:
        for n in range(2):
            for q in range(4):
                pltpu.make_async_copy(
                    forcing.at[n, :, x, :, pl.ds(q * 128, 128)],
                    F.at[x, :, :, n * 4 + q, :], ld_f.at[x],
                ).start()

    zero16 = jnp.zeros((comps, 16, 8, 128), jnp.float32)
    zero1 = jnp.zeros((comps, 8, 128), jnp.float32)
    zero4 = jnp.zeros((comps, 4, 8, 128), jnp.float32)
    zero8 = jnp.zeros((comps, 8, 8, 128), jnp.float32)
    zend = 17 * co
    zend_c = 9 * co

    for x in range(8):
        for buf in (S, A, B):
            buf[x + 1, :, zend] = zero1
    for x in range(4):
        E1[x + 1, :, zend_c] = zero1

    @pl.when(sp == 0)
    def _():
        for buf in (S, A, B):
            buf[0, :, pl.ds(1, 16)] = zero16
        E1[0, :, pl.ds(1, 8)] = zero8
        XI[0, 1] = zero4

    @pl.when(sp == spaces - 1)
    def _():
        for buf in (S, A, B):
            buf[9, :, pl.ds(1, 16)] = zero16
        E1[5, :, pl.ds(1, 8)] = zero8
        XI[0, 0] = zero4

    bar = pltpu.get_barrier_semaphore()
    for r in (1, 2, 3):
        pl.semaphore_signal(bar, inc=1, device_id={"instance": lax.rem(it + r, 4)}, device_id_type=MESH)
    pl.semaphore_signal(bar, inc=1, device_id={"coarse": 1 - co}, device_id_type=MESH)

    @pl.when(has_lo)
    def _():
        pl.semaphore_signal(bar, inc=1, device_id={"space": sp - 1}, device_id_type=MESH)

    @pl.when(has_hi)
    def _():
        pl.semaphore_signal(bar, inc=1, device_id={"space": sp + 1}, device_id_type=MESH)

    pl.semaphore_wait(bar, 4 + has_lo.astype(jnp.int32) + has_hi.astype(jnp.int32))

    def level_range(level, s):
        back = max(level - 1, 0)
        return (CUTS[s] - back if s > 0 else 0, CUTS[s + 1] - back if s < SLABS - 1 else 16)

    def level_buf(level):
        return (S, A, B)[level % 3]

    def xface(level, s, side):
        d0, d1 = level_range(level, s)
        z0 = 1 + zrange(d0, d1)
        buf = level_buf(level)
        i = ((level % 3) * SLABS + s) * 2 + side
        return pltpu.make_async_remote_copy(
            buf.at[1 if side == 0 else 8, :, pl.ds(z0, d1 - d0)],
            buf.at[9 if side == 0 else 0, :, pl.ds(z0, d1 - d0)],
            xs_s.at[i], xs_r.at[i],
            device_id={"space": sp - 1 if side == 0 else sp + 1}, device_id_type=MESH,
        )

    def x_send(level, s):
        pl.when(has_lo)(lambda: xface(level, s, 0).start())
        pl.when(has_hi)(lambda: xface(level, s, 1).start())

    def x_sent(level, s):
        pl.when(has_lo)(lambda: xface(level, s, 0).wait_send())
        pl.when(has_hi)(lambda: xface(level, s, 1).wait_send())

    def x_recv(level, s):
        pl.when(has_hi)(lambda: xface(level, s, 0).wait_recv())
        pl.when(has_lo)(lambda: xface(level, s, 1).wait_recv())

    def zface(level, x):
        buf = level_buf(level)
        i = (level % 3) * 8 + x
        return pltpu.make_async_remote_copy(
            buf.at[x + 1, :, pl.ds(16 - 15 * co, 1)], buf.at[x + 1, :, pl.ds(17 * co, 1)],
            zs_s.at[i], zs_r.at[i], device_id={"coarse": 1 - co}, device_id_type=MESH,
        )

    def planes(q):
        t = q % 4
        return ((t, pa, pb), (7 - t, pb, pa))

    def chunk(q):
        d0, d1 = CUTS[q // 4], CUTS[q // 4 + 1]
        return zrange(d0, d1), d1 - d0

    def raw(q, x, partner):
        z0, n = chunk(q)
        i = q * 2 + (0 if x < 4 else 1)
        return pltpu.make_async_remote_copy(
            S.at[x + 1, :, pl.ds(1 + z0, n)], R1.at[x, :, pl.ds(z0, n)],
            p1s.at[i], p1r.at[i], device_id={"instance": partner}, device_id_type=MESH,
        )

    def sums(q, x, partner):
        z0, n = chunk(q)
        i = q * 2 + (0 if x < 4 else 1)
        return pltpu.make_async_remote_copy(
            C2.at[x, :, pl.ds(z0, n)], R2.at[x, :, pl.ds(z0, n)],
            p2s.at[i], p2r.at[i], device_id={"instance": partner}, device_id_type=MESH,
        )

    def raw_start(q):
        for x, first, second in planes(q):
            raw(q, x, first).start()

    for x in order:
        view = S.at[x + 1, :, pl.ds(1, 16)]
        pltpu.make_async_copy(view, view, ld_s.at[x]).wait()
        if x >= 4 and 7 - x < LOOKAHEAD:
            raw_start(7 - x)
    for s in range(SLABS):
        x_send(0, s)
    for x in order:
        zface(0, x).start()

    def pack(z, carry):
        for c in range(comps):
            for xh in range(2):
                total = E[c, xh]
                for xq in range(4):
                    v = pltpu.roll(S[xh * 4 + xq + 1, c, z + 1], xq * 32 + 2 * z + 1, 1)
                    total = jnp.where((lane // 2) == xq * 16 + z, v, total)
                E[c, xh] = total
        return carry

    E[...] = jnp.zeros_like(E)
    lax.fori_loop(0, 16, pack, 0)

    def edge(r):
        return pltpu.make_async_remote_copy(
            E, EG.at[r - 1], es.at[r - 1], er.at[r - 1],
            device_id={"instance": lax.rem(it + r, 4)}, device_id_type=MESH,
        )

    for r in (1, 2, 3):
        edge(r).start()

    pltpu.make_async_copy(K, K, ld_k.at[0]).wait()
    even_lane = lane % 2 == 0

    def pair_sum(v):
        return v + jnp.where(even_lane, turn(v, 127, 1), turn(v, 1, 1))

    def steps(i, carry):
        z = i * 4
        for xc in range(4):
            k0, k1 = K[2 * xc, pl.ds(z, 4)], K[2 * xc + 1, pl.ds(z, 4)]
            W[2 * xc, pl.ds(z, 4)] = 0.8 / (6.0 + k0)
            W[2 * xc + 1, pl.ds(z, 4)] = 0.8 / (6.0 + k1)
            total = (k0 + k1).reshape(2, 2, 8, 128)
            WC[xc, pl.ds(2 * i, 2)] = 0.8 / (6.0 + pair_sum(total[:, 0] + total[:, 1]) * 0.125)
        return carry

    lax.fori_loop(0, 4, steps, 0)

    for x in order:
        view = F.at[x]
        pltpu.make_async_copy(view, view, ld_f.at[x]).wait()

    def ghosts():
        zl = (lane % 32) // 2
        lags = jnp.zeros((8, 128), jnp.int32)
        for z in range(16):
            lags = jnp.where(zl == z, lag[z], lags)
        mine = 2 * it + inst
        low = (mine - lags + 8) % 8
        high = (mine + lags) % 8
        want = jnp.where(
            (quarter == 0) & (lane % 2 == 1), low, jnp.where((quarter == 3) & (lane % 2 == 0), high, -1)
        )
        low_slot = lane % 2 == 1
        for r in (1, 2, 3):
            edge(r).wait_recv()
        for c in range(comps):
            for xh in range(2):
                total = jnp.zeros((8, 128), jnp.float32)
                for r in range(4):
                    p = E[c, xh] if r == 0 else EG[r - 1, c, xh]
                    who = lax.rem(it + 4 - r, 4)
                    up, down = pltpu.roll(p, 1, 1), pltpu.roll(p, 127, 1)
                    same = jnp.where(low_slot, pltpu.roll(up, 5, 0), pltpu.roll(down, 3, 0))
                    other = jnp.where(low_slot, pltpu.roll(up, 1, 0), pltpu.roll(down, 7, 0))
                    total = jnp.where(want == 2 * who + inst, same, total)
                    total = jnp.where(want == 2 * who + 1 - inst, other, total)
                GP[c, xh] = total

        ends = ((lane == 0) & (quarter == 0)) | ((lane == 127) & (quarter == 3))

        def unpack(z, carry):
            for xh in range(2):
                for c in range(comps):
                    g = GP[c, xh]
                    for xq in range(4):
                        x = xh * 4 + xq
                        v = pltpu.roll(g, 127 - xq * 32 - 2 * z, 1)
                        F[x, c, z] = F[x, c, z] + jnp.where(ends, v, 0.0)
            return carry

        lax.fori_loop(0, 16, unpack, 0)

    def by_inst(v0, v1):
        return jnp.where(inst == 0, v0, v1).astype(jnp.float32)

    delta = by_inst(-D1, D1)
    gamma = by_inst(D3, -D3)
    plus = by_inst(D1, D3)
    minus = by_inst(-D3, -D1)

    def source_part(q):
        z0, n = chunk(q)
        for x, first, second in planes(q):
            raw(q, x, first).wait_recv()
        for x, first, second in planes(q):
            up = odd == (1 if x < 4 else 0)
            alpha = jnp.where(up, D2, -D2).astype(jnp.float32)
            beta = jnp.where(up, plus, minus)

            def part(i, carry):
                z = z0 + i * WIDE
                for c in range(comps):
                    u, v = S[x + 1, c, pl.ds(z + 1, WIDE)], R1[x, c, pl.ds(z, WIDE)]
                    ur, vr = turn(u, 4, 0), turn(v, 4, 0)
                    C2[x, c, pl.ds(z, WIDE)] = (alpha * u + beta * ur) + (D4 * v + gamma * vr)
                    F[x, c, pl.ds(z, WIDE)] = F[x, c, pl.ds(z, WIDE)] - (delta * ur + (alpha * v + beta * vr))
                return carry

            lax.fori_loop(0, n // WIDE, part, 0)
            sums(q, x, second).start()

    def source_rest(q):
        z0, n = chunk(q)
        for x, first, second in planes(q):
            sums(q, x, second).wait_recv()
            raw(q, x, first).wait_send()

        def rest(i, carry):
            z = pl.ds(z0 + i * WIDE, WIDE)
            for x, first, second in planes(q):
                for c in range(comps):
                    F[x, c, z] = F[x, c, z] - R2[x, c, z]
            return carry

        lax.fori_loop(0, n // WIDE, rest, 0)

    lane_lo, lane_hi = lane == 0, lane == 127
    fix_lo = lane_lo & (quarter != 0)
    fix_hi = lane_hi & (quarter != 3)

    def pick(mask, a, b):
        return jnp.where(jnp.broadcast_to(mask, a.shape), a, b)

    def beside_y(u):
        lo, hi = turn(u, 1, 1), turn(u, 127, 1)
        zero = jnp.zeros_like(u)
        lower = pick(fix_lo, turn(lo, 1, 0), pick(lane_lo, zero, lo))
        upper = pick(fix_hi, turn(hi, 7, 0), pick(lane_hi, zero, hi))
        return lower + upper

    def mix(us, c):
        total = coupling[c, 0] * us[0]
        for d in range(1, comps):
            total = total + coupling[c, d] * us[d]
        return total

    def balance(buf, x, z, n):
        us = [buf[x + 1, c, pl.ds(z + 1, n)] for c in range(comps)]
        ys = [beside_y(u) for u in us]
        got = []
        for c in range(comps):
            near = (buf[x, c, pl.ds(z + 1, n)] + buf[x + 2, c, pl.ds(z + 1, n)]) + (
                buf[x + 1, c, pl.ds(z, n)] + buf[x + 1, c, pl.ds(z + 2, n)]
            )
            got.append((F[x, c, pl.ds(z, n)] + near) + (ys[c] - mix(us, c)))
        return us, got

    def stage_cells(k, j, z, n):
        src, dst, weight = level_buf(k - 1), level_buf(k), WEIGHTS[(k - 1) % 3]
        for x in (j, 7 - j):
            us, got = balance(src, x, z, n)
            w = W[x, pl.ds(z, n)] * weight
            for c in range(comps):
                own = us[c] if src is S else S[x + 1, c, pl.ds(z + 1, n)]
                dst[x + 1, c, pl.ds(z + 1, n)] = (own - (0.8 * weight) * us[c]) + w * got[c]

    def last_cells(j, z, n):
        half = z // 2
        for x in (j, 7 - j):
            us, got = balance(S, x, z, n)
            diag = 6.0 + K[x, pl.ds(z, n)]
            for c in range(comps):
                res = (got[c] - diag * us[c]).reshape(n // 2, 2, 8, 128)
                total = res[:, 0] + res[:, 1]
                if j % 2 == 1:
                    total = total + RHS[x // 2, c, pl.ds(half, n // 2)]
                RHS[x // 2, c, pl.ds(half, n // 2)] = total

    def run(k, j, s):
        if j == 0 and k <= STAGES:
            x_recv(k - 1, s)
            if k >= 3:
                x_sent(k - 3, s)
        if s == 0 and k <= STAGES:
            for x in (j, 7 - j):
                zface(k - 1, x).wait_recv()
                if k >= 3:
                    zface(k - 3, x).wait_send()
        d0, d1 = level_range(k, s)
        z0, n = zrange(d0, d1), d1 - d0
        cells = functools.partial(stage_cells, k) if k <= STAGES else last_cells
        wide, rest = divmod(n, WIDE)

        def many(i, carry):
            cells(j, z0 + i * WIDE, WIDE)
            return carry

        if wide:
            lax.fori_loop(0, wide, many, 0)
        if rest:
            cells(j, z0 + wide * WIDE, rest)
        if k < STAGES:
            if j == 0:
                x_send(k, s)
            if s == 0:
                for x in (j, 7 - j):
                    zface(k, x).start()
        if k == 4:
            if j == 0:
                for x in (0, 9):
                    S[x, :, pl.ds(1 + z0, n)] = jnp.zeros((comps, n, 8, 128), jnp.float32)
            if s == 0:
                for x in (j, 7 - j):
                    S[x + 1, :, 17 * (1 - co)] = zero1
        if k == STAGES:
            if j == 0 and s == SLABS - 1:
                smooth_x()
            if j % 2 == 1 and s == 0:
                smooth_z(j // 2)

    def wave(t, s):
        for k in range(max(1, t - 2), min(STAGES + 1, t + 1) + 1):
            run(k, t + 1 - k, s)

    def px(kind, side):
        return pltpu.make_async_remote_copy(
            XO.at[kind, side], XI.at[kind, side], px_s.at[kind * 2 + side], px_r.at[kind * 2 + side],
            device_id={"space": sp - 1 if side == 0 else sp + 1}, device_id_type=MESH,
        )

    def px_start(kind):
        pl.when(has_lo)(lambda: px(kind, 0).start())
        pl.when(has_hi)(lambda: px(kind, 1).start())

    def px_sent(kind):
        pl.when(has_lo)(lambda: px(kind, 0).wait_send())
        pl.when(has_hi)(lambda: px(kind, 1).wait_send())

    def px_recv(kind):
        pl.when(has_hi)(lambda: px(kind, 0).wait_recv())
        pl.when(has_lo)(lambda: px(kind, 1).wait_recv())

    def pz(kind, group):
        i = kind * 2 + group
        return pltpu.make_async_remote_copy(
            ZO.at[kind, group], ZI.at[kind, group], pz_s.at[i], pz_r.at[i],
            device_id={"coarse": 1 - co}, device_id_type=MESH,
        )

    def join(first, second):
        return pick(even_lane, first + turn(first, 127, 1), second + turn(second, 1, 1))

    def smooth_x():
        for side, x in ((0, 1), (1, 8)):
            for c in range(comps):
                v = S[x, c, pl.ds(1, 16)].reshape(4, 2, 2, 8, 128)
                v = v[:, :, 0] + v[:, :, 1]
                XO[0, side, c] = join(v[:, 0], v[:, 1])
        px_start(0)

    def smooth_z(group):
        zi = 16 - 15 * co
        for c in range(comps):
            v = [S[2 * xc + 1, c, zi] + S[2 * xc + 2, c, zi] for xc in (group, 3 - group)]
            ZO[0, group, c] = join(v[0], v[1])
        pz(0, group).start()

    zc_in = 7 * (1 - co)

    def first_sweep(group):
        pz(0, group).wait_recv()
        if group == 0:
            px_recv(0)
        for i, xc in enumerate((group, 3 - group)):
            mask = even_lane if i == 0 else ~even_lane
            for c in range(comps):
                RHS[xc, c, zc_in] = RHS[xc, c, zc_in] + jnp.where(mask, ZI[0, group, c], 0.0)
        for xc in (group, 3 - group):
            for c in range(comps):
                rhs = RHS[xc, c]
                if group == 0:
                    got = XI[0, 1 if xc == 0 else 0, c]
                    none = jnp.zeros_like(got)
                    rhs = rhs + jnp.stack([pick(even_lane, got, none), pick(even_lane, none, got)], 1).reshape(8, 8, 128)
                E1[xc + 1, c, pl.ds(1, 8)] = WC[xc] * pair_sum(rhs)
        if group == 0:
            for side, xc in ((0, 0), (1, 3)):
                for c in range(comps):
                    v = E1[xc + 1, c, pl.ds(1, 8)].reshape(4, 2, 8, 128)
                    XO[1, side, c] = pick(even_lane, v[:, 0], v[:, 1])
            px_start(1)
        for c in range(comps):
            ZO[1, group, c] = jnp.where(even_lane, E1[group + 1, c, 1 + zc_in], E1[4 - group, c, 1 + zc_in])
        pz(1, group).start()

    def coarse_halo(group):
        pz(1, group).wait_recv()
        for c in range(comps):
            v = ZI[1, group, c]
            E1[group + 1, c, 9 * (1 - co)] = jnp.where(even_lane, v, pltpu.roll(v, 1, 1))
            E1[4 - group, c, 9 * (1 - co)] = jnp.where(even_lane, pltpu.roll(v, 127, 1), v)
        if group == 0:

            def unpack(side, x):
                for c in range(comps):
                    v = XI[1, side, c]
                    e0, e1 = pick(even_lane, v, turn(v, 1, 1)), pick(even_lane, turn(v, 127, 1), v)
                    E1[x, c, pl.ds(1, 8)] = jnp.stack([e0, e1], 1).reshape(8, 8, 128)

            px_recv(1)
            pl.when(has_hi)(lambda: unpack(0, 5))
            pl.when(has_lo)(lambda: unpack(1, 0))

    lo2, hi2 = lane < 2, lane >= 126
    first_q, last_q = quarter == 0, quarter == 3

    def beside_y2(u):
        lo, hi = turn(u, 2, 1), turn(u, 126, 1)
        wrap_lo = pick(first_q, turn(lo, 5, 0), turn(lo, 1, 0))
        wrap_hi = pick(last_q, turn(hi, 3, 0), turn(hi, 7, 0))
        return pick(lo2, wrap_lo, lo) + pick(hi2, wrap_hi, hi)

    def second_sweep(xc):
        def body(i, carry):
            z = i * 4
            mid = pl.ds(z + 1, 4)
            ee = [E1[xc + 1, c, mid] for c in range(comps)]
            w = WC[xc, pl.ds(z, 4)]
            for c in range(comps):
                near = (E1[xc, c, mid] + E1[xc + 2, c, mid]) + (
                    E1[xc + 1, c, pl.ds(z, 4)] + E1[xc + 1, c, pl.ds(z + 2, 4)]
                )
                e = 1.2 * ee[c] + w * ((near + beside_y2(ee[c])) - mix(ee, c))
                fine = jnp.broadcast_to(e[:, None], (4, 2, 8, 128)).reshape(8, 8, 128)
                for x in (2 * xc, 2 * xc + 1):
                    at = pl.ds(2 * z + 1, 8)
                    S[x + 1, c, at] = S[x + 1, c, at] + fine
            return carry

        lax.fori_loop(0, 2, body, 0)
        for x in (2 * xc, 2 * xc + 1):
            for n in range(2):
                for q in range(4):
                    pltpu.make_async_copy(
                        S.at[x + 1, :, pl.ds(1, 16), n * 4 + q, :],
                        out.at[n, :, x, :, pl.ds(q * 128, 128)], out_sem.at[x],
                    ).start()

    def chunk_in(q):
        source_part(q)
        if q + LOOKAHEAD < CHUNKS:
            raw_start(q + LOOKAHEAD)

    chunk_in(0)
    ghosts()
    for q in range(CHUNKS):
        if q + 1 < CHUNKS:
            chunk_in(q + 1)
        source_rest(q)
        s, t = divmod(q, 4)
        wave(t, s)
        if s > 0:
            if t < 3:
                wave(4 + t, s - 1)
            else:
                for later in (7, 8, 9):
                    wave(later, s - 1)
    for t in range(4, 8):
        wave(t, SLABS - 1)
    first_sweep(0)
    wave(8, SLABS - 1)
    wave(9, SLABS - 1)
    first_sweep(1)
    coarse_halo(1)
    second_sweep(1)
    second_sweep(2)
    coarse_halo(0)
    second_sweep(0)
    second_sweep(3)

    for level in (4, 5):
        for s in range(SLABS):
            x_sent(level, s)
        for x in range(8):
            zface(level, x).wait_send()
    for q in range(CHUNKS):
        for x, first, second in planes(q):
            sums(q, x, second).wait_send()
    for r in (1, 2, 3):
        edge(r).wait_send()
    for kind in range(2):
        px_sent(kind)
        for group in range(2):
            pz(kind, group).wait_send()
    for x in range(8):
        view = S.at[x + 1, :, pl.ds(1, 16)]
        pltpu.make_async_copy(view, view, out_sem.at[x]).wait()


def leg(forcing, start, kappa, coupling, lag):
    f32 = jnp.float32
    vmem = pltpu.VMEM
    dma = pltpu.SemaphoreType.DMA
    hbm = pl.BlockSpec(memory_space=pltpu.HBM)
    smem = pl.BlockSpec(memory_space=pltpu.SMEM)
    block = (8, 5, 16, 8, 128)
    halo = (10, 5, 18, 8, 128)
    return pl.pallas_call(
        leg_kernel,
        out_shape=jax.ShapeDtypeStruct(start.shape, f32),
        in_specs=[hbm, hbm, hbm, smem, smem],
        out_specs=hbm,
        scratch_shapes=[
            vmem(halo, f32), vmem(halo, f32), vmem(halo, f32),
            vmem(block, f32), vmem(block, f32), vmem(block, f32), vmem(block, f32),
            vmem((8, 16, 8, 128), f32), vmem((8, 16, 8, 128), f32),
            vmem((5, 2, 8, 128), f32), vmem((3, 5, 2, 8, 128), f32), vmem((5, 2, 8, 128), f32),
            vmem((4, 5, 8, 8, 128), f32), vmem((4, 8, 8, 128), f32),
            vmem((6, 5, 10, 8, 128), f32),
            vmem((2, 2, 5, 4, 8, 128), f32), vmem((2, 2, 5, 4, 8, 128), f32),
            vmem((2, 2, 5, 8, 128), f32), vmem((2, 2, 5, 8, 128), f32),
            dma((8,)), dma((8,)), dma((1,)),
            dma((2 * CHUNKS,)), dma((2 * CHUNKS,)), dma((2 * CHUNKS,)), dma((2 * CHUNKS,)),
            dma((3,)), dma((3,)),
            dma((6 * SLABS,)), dma((6 * SLABS,)), dma((24,)), dma((24,)),
            dma((4,)), dma((4,)), dma((4,)), dma((4,)), dma((8,)),
        ],
        compiler_params=pltpu.CompilerParams(
            collective_id=0, has_side_effects=True, vmem_limit_bytes=56 * 2**20
        ),
        name="leg",
    )(forcing, start, kappa, coupling, lag)


def shards(forcing, state_start, kappa, coupling, lag):
    return leg(forcing, state_start, kappa, coupling, lag)


def solution(mesh):
    return jax.shard_map(
        shards,
        mesh=mesh,
        in_specs=(
            P("instance", None, "space", "coarse", None),
            P("instance", None, "space", "coarse", None),
            P("space", "coarse", None),
            P(),
            P("coarse"),
        ),
        out_specs=P("instance", None, "space", "coarse", None),
        check_vma=False,
    )
```

```python
import functools
import math

import jax
import jax.numpy as jnp
import numpy as np
from jax import lax
from jax.experimental import pallas as pl
from jax.experimental.pallas import tpu as pltpu
from jax.sharding import PartitionSpec as P

MESH = pl.DeviceIdType.MESH
WEIGHTS = (0.25, 0.5, 1.0)
STAGES = 6
CUTS = (0, 8, 12, 16)
SLABS = len(CUTS) - 1
CHUNKS = 4 * SLABS
ORDER = ((0, 0), (1, 0), (0, 1), (2, 0), (1, 1), (0, 2), (3, 0), (2, 1), (1, 2), (3, 1), (2, 2), (3, 2))
LATER = {(2, 1): ((4, 0),), (3, 1): ((5, 0),), (2, 2): ((4, 1), (6, 0)), (3, 2): ((5, 1), (7, 0))}
ENDING = ((4, 2), (6, 1), (8, 0), (9, 0), (5, 2), (7, 1), (6, 2), (8, 1), (9, 1), (7, 2))
LOOKAHEAD = 2
WIDE = 4


def spectral(d):
    if d == 0:
        return 0.0
    return float(0.5 * (-1.0) ** abs(d) * math.cos(math.pi * d / 8) / math.sin(math.pi * d / 8))


D1, D2, D3, D4 = spectral(1), spectral(2), spectral(3), spectral(4)


def leg_kernel(
    forcing, start, kappa, coupling, lag, out,
    S, A, B, F, R1, C2, R2, K, W, E, EG, GP, RHS, WC, E1, XO, XI, ZO, ZI,
    ld_s, ld_f, ld_k, p1s, p1r, p2s, p2r, es, er, xs_s, xs_r, zs_s, zs_r, px_s, px_r, pz_s, pz_r, out_sem,
):
    comps = 5
    sp, it, co = lax.axis_index("space"), lax.axis_index("instance"), lax.axis_index("coarse")
    spaces = lax.axis_size("space")
    odd = lax.rem(it, 2)
    pa = lax.rem(it + 1 + 2 * odd, 4)
    pb = lax.rem(it + 3 + 2 * odd, 4)
    has_lo, has_hi = sp > 0, sp < spaces - 1

    sub = lax.broadcasted_iota(jnp.int32, (8, 128), 0)
    lane = lax.broadcasted_iota(jnp.int32, (8, 128), 1)
    inst = sub // 4
    quarter = sub % 4

    def zrange(d0, d1):
        return (1 - co) * (16 - d1) + co * d0

    def turn(v, shift, axis):
        if v.ndim == 2:
            return pltpu.roll(v, shift, axis)
        if axis == 1:
            return pltpu.roll(v.reshape(-1, 128), shift, 1).reshape(v.shape)
        return jnp.stack([pltpu.roll(v[i], shift, 0) for i in range(v.shape[0])])

    order = (0, 7, 1, 6, 2, 5, 3, 4)
    for x in order:
        for n in range(2):
            for q in range(4):
                pltpu.make_async_copy(
                    start.at[n, :, x, :, pl.ds(q * 128, 128)],
                    S.at[x + 1, :, pl.ds(1, 16), n * 4 + q, :], ld_s.at[x],
                ).start()
    for n in range(2):
        for q in range(4):
            pltpu.make_async_copy(
                kappa.at[:, :, pl.ds(q * 128, 128)], K.at[:, :, n * 4 + q, :], ld_k.at[0]
            ).start()
    for x in order:
        for n in range(2):
            for q in range(4):
                pltpu.make_async_copy(
                    forcing.at[n, :, x, :, pl.ds(q * 128, 128)],
                    F.at[x, :, :, n * 4 + q, :], ld_f.at[x],
                ).start()

    zero16 = jnp.zeros((comps, 16, 8, 128), jnp.float32)
    zero1 = jnp.zeros((comps, 8, 128), jnp.float32)
    zero4 = jnp.zeros((comps, 4, 8, 128), jnp.float32)
    zero8 = jnp.zeros((comps, 8, 8, 128), jnp.float32)
    zend = 17 * co
    zend_c = 9 * co

    for x in range(8):
        for buf in (S, A, B):
            buf[x + 1, :, zend] = zero1
    for x in range(4):
        E1[x + 1, :, zend_c] = zero1

    @pl.when(sp == 0)
    def _():
        for buf in (S, A, B):
            buf[0, :, pl.ds(1, 16)] = zero16
        E1[0, :, pl.ds(1, 8)] = zero8
        XI[0, 1] = zero4

    @pl.when(sp == spaces - 1)
    def _():
        for buf in (S, A, B):
            buf[9, :, pl.ds(1, 16)] = zero16
        E1[5, :, pl.ds(1, 8)] = zero8
        XI[0, 0] = zero4

    bar = pltpu.get_barrier_semaphore()
    for r in (1, 2, 3):
        pl.semaphore_signal(bar, inc=1, device_id={"instance": lax.rem(it + r, 4)}, device_id_type=MESH)
    pl.semaphore_signal(bar, inc=1, device_id={"coarse": 1 - co}, device_id_type=MESH)

    @pl.when(has_lo)
    def _():
        pl.semaphore_signal(bar, inc=1, device_id={"space": sp - 1}, device_id_type=MESH)

    @pl.when(has_hi)
    def _():
        pl.semaphore_signal(bar, inc=1, device_id={"space": sp + 1}, device_id_type=MESH)

    pl.semaphore_wait(bar, 4 + has_lo.astype(jnp.int32) + has_hi.astype(jnp.int32))

    def level_range(level, s):
        back = max(level - 1, 0)
        return (CUTS[s] - back if s > 0 else 0, CUTS[s + 1] - back if s < SLABS - 1 else 16)

    def level_buf(level):
        return (S, A, B)[level % 3]

    def xface(level, s, side):
        d0, d1 = level_range(level, s)
        z0 = 1 + zrange(d0, d1)
        buf = level_buf(level)
        i = ((level % 3) * SLABS + s) * 2 + side
        return pltpu.make_async_remote_copy(
            buf.at[1 if side == 0 else 8, :, pl.ds(z0, d1 - d0)],
            buf.at[9 if side == 0 else 0, :, pl.ds(z0, d1 - d0)],
            xs_s.at[i], xs_r.at[i],
            device_id={"space": sp - 1 if side == 0 else sp + 1}, device_id_type=MESH,
        )

    def x_send(level, s):
        pl.when(has_lo)(lambda: xface(level, s, 0).start())
        pl.when(has_hi)(lambda: xface(level, s, 1).start())

    def x_sent(level, s):
        pl.when(has_lo)(lambda: xface(level, s, 0).wait_send())
        pl.when(has_hi)(lambda: xface(level, s, 1).wait_send())

    def x_recv(level, s):
        pl.when(has_hi)(lambda: xface(level, s, 0).wait_recv())
        pl.when(has_lo)(lambda: xface(level, s, 1).wait_recv())

    def zface(level, x):
        buf = level_buf(level)
        i = (level % 3) * 8 + x
        return pltpu.make_async_remote_copy(
            buf.at[x + 1, :, pl.ds(16 - 15 * co, 1)], buf.at[x + 1, :, pl.ds(17 * co, 1)],
            zs_s.at[i], zs_r.at[i], device_id={"coarse": 1 - co}, device_id_type=MESH,
        )

    def planes(q):
        t = q % 4
        return ((t, pa, pb), (7 - t, pb, pa))

    def chunk(q):
        d0, d1 = CUTS[q // 4], CUTS[q // 4 + 1]
        return zrange(d0, d1), d1 - d0

    def raw(q, x, partner):
        z0, n = chunk(q)
        i = q * 2 + (0 if x < 4 else 1)
        return pltpu.make_async_remote_copy(
            S.at[x + 1, :, pl.ds(1 + z0, n)], R1.at[x, :, pl.ds(z0, n)],
            p1s.at[i], p1r.at[i], device_id={"instance": partner}, device_id_type=MESH,
        )

    def sums(q, x, partner):
        z0, n = chunk(q)
        i = q * 2 + (0 if x < 4 else 1)
        return pltpu.make_async_remote_copy(
            C2.at[x, :, pl.ds(z0, n)], R2.at[x, :, pl.ds(z0, n)],
            p2s.at[i], p2r.at[i], device_id={"instance": partner}, device_id_type=MESH,
        )

    def raw_start(q):
        for x, first, second in planes(q):
            raw(q, x, first).start()

    for x in order:
        view = S.at[x + 1, :, pl.ds(1, 16)]
        pltpu.make_async_copy(view, view, ld_s.at[x]).wait()
        for t, s in ORDER[:LOOKAHEAD]:
            if t == 7 - x:
                raw_start(s * 4 + t)
    for s in range(SLABS):
        x_send(0, s)
    for x in order:
        zface(0, x).start()

    def pack(z, carry):
        for c in range(comps):
            for xh in range(2):
                total = E[c, xh]
                for xq in range(4):
                    v = pltpu.roll(S[xh * 4 + xq + 1, c, z + 1], xq * 32 + 2 * z + 1, 1)
                    total = jnp.where((lane // 2) == xq * 16 + z, v, total)
                E[c, xh] = total
        return carry

    E[...] = jnp.zeros_like(E)
    lax.fori_loop(0, 16, pack, 0)

    def edge(r):
        return pltpu.make_async_remote_copy(
            E, EG.at[r - 1], es.at[r - 1], er.at[r - 1],
            device_id={"instance": lax.rem(it + r, 4)}, device_id_type=MESH,
        )

    for r in (1, 2, 3):
        edge(r).start()

    pltpu.make_async_copy(K, K, ld_k.at[0]).wait()
    even_lane = lane % 2 == 0

    def pair_sum(v):
        return v + jnp.where(even_lane, turn(v, 127, 1), turn(v, 1, 1))

    def steps(i, carry):
        z = i * 4
        for xc in range(4):
            k0, k1 = K[2 * xc, pl.ds(z, 4)], K[2 * xc + 1, pl.ds(z, 4)]
            W[2 * xc, pl.ds(z, 4)] = 0.8 / (6.0 + k0)
            W[2 * xc + 1, pl.ds(z, 4)] = 0.8 / (6.0 + k1)
            total = (k0 + k1).reshape(2, 2, 8, 128)
            WC[xc, pl.ds(2 * i, 2)] = 0.8 / (6.0 + pair_sum(total[:, 0] + total[:, 1]) * 0.125)
        return carry

    lax.fori_loop(0, 4, steps, 0)

    for x in order:
        view = F.at[x]
        pltpu.make_async_copy(view, view, ld_f.at[x]).wait()

    def ghosts():
        zl = (lane % 32) // 2
        lags = jnp.zeros((8, 128), jnp.int32)
        for z in range(16):
            lags = jnp.where(zl == z, lag[z], lags)
        mine = 2 * it + inst
        low = (mine - lags + 8) % 8
        high = (mine + lags) % 8
        want = jnp.where(
            (quarter == 0) & (lane % 2 == 1), low, jnp.where((quarter == 3) & (lane % 2 == 0), high, -1)
        )
        low_slot = lane % 2 == 1
        for r in (1, 2, 3):
            edge(r).wait_recv()
        for c in range(comps):
            for xh in range(2):
                total = jnp.zeros((8, 128), jnp.float32)
                for r in range(4):
                    p = E[c, xh] if r == 0 else EG[r - 1, c, xh]
                    who = lax.rem(it + 4 - r, 4)
                    up, down = pltpu.roll(p, 1, 1), pltpu.roll(p, 127, 1)
                    same = jnp.where(low_slot, pltpu.roll(up, 5, 0), pltpu.roll(down, 3, 0))
                    other = jnp.where(low_slot, pltpu.roll(up, 1, 0), pltpu.roll(down, 7, 0))
                    total = jnp.where(want == 2 * who + inst, same, total)
                    total = jnp.where(want == 2 * who + 1 - inst, other, total)
                GP[c, xh] = total

        ends = ((lane == 0) & (quarter == 0)) | ((lane == 127) & (quarter == 3))

        def unpack(z, carry):
            for xh in range(2):
                for c in range(comps):
                    g = GP[c, xh]
                    for xq in range(4):
                        x = xh * 4 + xq
                        v = pltpu.roll(g, 127 - xq * 32 - 2 * z, 1)
                        F[x, c, z] = F[x, c, z] + jnp.where(ends, v, 0.0)
            return carry

        lax.fori_loop(0, 16, unpack, 0)

    def by_inst(v0, v1):
        return jnp.where(inst == 0, v0, v1).astype(jnp.float32)

    delta = by_inst(-D1, D1)
    gamma = by_inst(D3, -D3)
    plus = by_inst(D1, D3)
    minus = by_inst(-D3, -D1)

    def source_part(q):
        z0, n = chunk(q)
        for x, first, second in planes(q):
            raw(q, x, first).wait_recv()
        for x, first, second in planes(q):
            up = odd == (1 if x < 4 else 0)
            alpha = jnp.where(up, D2, -D2).astype(jnp.float32)
            beta = jnp.where(up, plus, minus)

            def part(i, carry):
                z = z0 + i * WIDE
                for c in range(comps):
                    u, v = S[x + 1, c, pl.ds(z + 1, WIDE)], R1[x, c, pl.ds(z, WIDE)]
                    ur, vr = turn(u, 4, 0), turn(v, 4, 0)
                    C2[x, c, pl.ds(z, WIDE)] = (alpha * u + beta * ur) + (D4 * v + gamma * vr)
                    F[x, c, pl.ds(z, WIDE)] = F[x, c, pl.ds(z, WIDE)] - (delta * ur + (alpha * v + beta * vr))
                return carry

            lax.fori_loop(0, n // WIDE, part, 0)
            sums(q, x, second).start()

    def source_rest(q):
        z0, n = chunk(q)
        for x, first, second in planes(q):
            sums(q, x, second).wait_recv()
            raw(q, x, first).wait_send()

        def rest(i, carry):
            z = pl.ds(z0 + i * WIDE, WIDE)
            for x, first, second in planes(q):
                for c in range(comps):
                    F[x, c, z] = F[x, c, z] - R2[x, c, z]
            return carry

        lax.fori_loop(0, n // WIDE, rest, 0)

    lane_lo, lane_hi = lane == 0, lane == 127
    fix_lo = lane_lo & (quarter != 0)
    fix_hi = lane_hi & (quarter != 3)

    def pick(mask, a, b):
        return jnp.where(jnp.broadcast_to(mask, a.shape), a, b)

    def beside_y(u):
        lo, hi = turn(u, 1, 1), turn(u, 127, 1)
        zero = jnp.zeros_like(u)
        lower = pick(fix_lo, turn(lo, 1, 0), pick(lane_lo, zero, lo))
        upper = pick(fix_hi, turn(hi, 7, 0), pick(lane_hi, zero, hi))
        return lower + upper

    def mix(us, c):
        total = coupling[c, 0] * us[0]
        for d in range(1, comps):
            total = total + coupling[c, d] * us[d]
        return total

    def balance(buf, x, z, n):
        us = [buf[x + 1, c, pl.ds(z + 1, n)] for c in range(comps)]
        ys = [beside_y(u) for u in us]
        got = []
        for c in range(comps):
            near = (buf[x, c, pl.ds(z + 1, n)] + buf[x + 2, c, pl.ds(z + 1, n)]) + (
                buf[x + 1, c, pl.ds(z, n)] + buf[x + 1, c, pl.ds(z + 2, n)]
            )
            got.append((F[x, c, pl.ds(z, n)] + near) + (ys[c] - mix(us, c)))
        return us, got

    def stage_cells(k, j, z, n):
        src, dst, weight = level_buf(k - 1), level_buf(k), WEIGHTS[(k - 1) % 3]
        for x in (j, 7 - j):
            us, got = balance(src, x, z, n)
            w = W[x, pl.ds(z, n)] * weight
            for c in range(comps):
                own = us[c] if src is S else S[x + 1, c, pl.ds(z + 1, n)]
                dst[x + 1, c, pl.ds(z + 1, n)] = (own - (0.8 * weight) * us[c]) + w * got[c]

    def last_cells(j, z, n):
        half = z // 2
        for x in (j, 7 - j):
            us, got = balance(S, x, z, n)
            diag = 6.0 + K[x, pl.ds(z, n)]
            for c in range(comps):
                res = (got[c] - diag * us[c]).reshape(n // 2, 2, 8, 128)
                total = res[:, 0] + res[:, 1]
                if j % 2 == 1:
                    total = total + RHS[x // 2, c, pl.ds(half, n // 2)]
                RHS[x // 2, c, pl.ds(half, n // 2)] = total

    def run(k, j, s):
        if j == 0 and k <= STAGES:
            x_recv(k - 1, s)
            if k >= 3:
                x_sent(k - 3, s)
        if s == 0 and k <= STAGES:
            for x in (j, 7 - j):
                zface(k - 1, x).wait_recv()
                if k >= 3:
                    zface(k - 3, x).wait_send()
        d0, d1 = level_range(k, s)
        z0, n = zrange(d0, d1), d1 - d0
        cells = functools.partial(stage_cells, k) if k <= STAGES else last_cells
        wide, rest = divmod(n, WIDE)

        def many(i, carry):
            cells(j, z0 + i * WIDE, WIDE)
            return carry

        if wide:
            lax.fori_loop(0, wide, many, 0)
        if rest:
            cells(j, z0 + wide * WIDE, rest)
        if k < STAGES:
            if j == 0:
                x_send(k, s)
            if s == 0:
                for x in (j, 7 - j):
                    zface(k, x).start()
        if k == 4:
            if j == 0:
                for x in (0, 9):
                    S[x, :, pl.ds(1 + z0, n)] = jnp.zeros((comps, n, 8, 128), jnp.float32)
            if s == 0:
                for x in (j, 7 - j):
                    S[x + 1, :, 17 * (1 - co)] = zero1
        if k == STAGES:
            if j == 0 and s == SLABS - 1:
                smooth_x()
            if j % 2 == 1 and s == 0:
                smooth_z(j // 2)

    def wave(t, s):
        for k in range(max(1, t - 2), min(STAGES + 1, t + 1) + 1):
            run(k, t + 1 - k, s)

    def px(kind, side):
        return pltpu.make_async_remote_copy(
            XO.at[kind, side], XI.at[kind, side], px_s.at[kind * 2 + side], px_r.at[kind * 2 + side],
            device_id={"space": sp - 1 if side == 0 else sp + 1}, device_id_type=MESH,
        )

    def px_start(kind):
        pl.when(has_lo)(lambda: px(kind, 0).start())
        pl.when(has_hi)(lambda: px(kind, 1).start())

    def px_sent(kind):
        pl.when(has_lo)(lambda: px(kind, 0).wait_send())
        pl.when(has_hi)(lambda: px(kind, 1).wait_send())

    def px_recv(kind):
        pl.when(has_hi)(lambda: px(kind, 0).wait_recv())
        pl.when(has_lo)(lambda: px(kind, 1).wait_recv())

    def pz(kind, group):
        i = kind * 2 + group
        return pltpu.make_async_remote_copy(
            ZO.at[kind, group], ZI.at[kind, group], pz_s.at[i], pz_r.at[i],
            device_id={"coarse": 1 - co}, device_id_type=MESH,
        )

    def join(first, second):
        return pick(even_lane, first + turn(first, 127, 1), second + turn(second, 1, 1))

    def smooth_x():
        for side, x in ((0, 1), (1, 8)):
            for c in range(comps):
                v = S[x, c, pl.ds(1, 16)].reshape(4, 2, 2, 8, 128)
                v = v[:, :, 0] + v[:, :, 1]
                XO[0, side, c] = join(v[:, 0], v[:, 1])
        px_start(0)

    def smooth_z(group):
        zi = 16 - 15 * co
        for c in range(comps):
            v = [S[2 * xc + 1, c, zi] + S[2 * xc + 2, c, zi] for xc in (group, 3 - group)]
            ZO[0, group, c] = join(v[0], v[1])
        pz(0, group).start()

    zc_in = 7 * (1 - co)

    def first_sweep(group):
        pz(0, group).wait_recv()
        if group == 0:
            px_recv(0)
        for i, xc in enumerate((group, 3 - group)):
            mask = even_lane if i == 0 else ~even_lane
            for c in range(comps):
                RHS[xc, c, zc_in] = RHS[xc, c, zc_in] + jnp.where(mask, ZI[0, group, c], 0.0)
        for xc in (group, 3 - group):
            for c in range(comps):
                rhs = RHS[xc, c]
                if group == 0:
                    got = XI[0, 1 if xc == 0 else 0, c]
                    none = jnp.zeros_like(got)
                    rhs = rhs + jnp.stack([pick(even_lane, got, none), pick(even_lane, none, got)], 1).reshape(8, 8, 128)
                E1[xc + 1, c, pl.ds(1, 8)] = WC[xc] * pair_sum(rhs)
        if group == 0:
            for side, xc in ((0, 0), (1, 3)):
                for c in range(comps):
                    v = E1[xc + 1, c, pl.ds(1, 8)].reshape(4, 2, 8, 128)
                    XO[1, side, c] = pick(even_lane, v[:, 0], v[:, 1])
            px_start(1)
        for c in range(comps):
            ZO[1, group, c] = jnp.where(even_lane, E1[group + 1, c, 1 + zc_in], E1[4 - group, c, 1 + zc_in])
        pz(1, group).start()

    def coarse_halo(group):
        pz(1, group).wait_recv()
        for c in range(comps):
            v = ZI[1, group, c]
            E1[group + 1, c, 9 * (1 - co)] = jnp.where(even_lane, v, pltpu.roll(v, 1, 1))
            E1[4 - group, c, 9 * (1 - co)] = jnp.where(even_lane, pltpu.roll(v, 127, 1), v)
        if group == 0:

            def unpack(side, x):
                for c in range(comps):
                    v = XI[1, side, c]
                    e0, e1 = pick(even_lane, v, turn(v, 1, 1)), pick(even_lane, turn(v, 127, 1), v)
                    E1[x, c, pl.ds(1, 8)] = jnp.stack([e0, e1], 1).reshape(8, 8, 128)

            px_recv(1)
            pl.when(has_hi)(lambda: unpack(0, 5))
            pl.when(has_lo)(lambda: unpack(1, 0))

    lo2, hi2 = lane < 2, lane >= 126
    first_q, last_q = quarter == 0, quarter == 3

    def beside_y2(u):
        lo, hi = turn(u, 2, 1), turn(u, 126, 1)
        wrap_lo = pick(first_q, turn(lo, 5, 0), turn(lo, 1, 0))
        wrap_hi = pick(last_q, turn(hi, 3, 0), turn(hi, 7, 0))
        return pick(lo2, wrap_lo, lo) + pick(hi2, wrap_hi, hi)

    def second_sweep(xc):
        def body(i, carry):
            z = i * 4
            mid = pl.ds(z + 1, 4)
            ee = [E1[xc + 1, c, mid] for c in range(comps)]
            w = WC[xc, pl.ds(z, 4)]
            for c in range(comps):
                near = (E1[xc, c, mid] + E1[xc + 2, c, mid]) + (
                    E1[xc + 1, c, pl.ds(z, 4)] + E1[xc + 1, c, pl.ds(z + 2, 4)]
                )
                e = 1.2 * ee[c] + w * ((near + beside_y2(ee[c])) - mix(ee, c))
                fine = jnp.broadcast_to(e[:, None], (4, 2, 8, 128)).reshape(8, 8, 128)
                for x in (2 * xc, 2 * xc + 1):
                    at = pl.ds(2 * z + 1, 8)
                    S[x + 1, c, at] = S[x + 1, c, at] + fine
            return carry

        lax.fori_loop(0, 2, body, 0)
        for x in (2 * xc, 2 * xc + 1):
            for n in range(2):
                for q in range(4):
                    pltpu.make_async_copy(
                        S.at[x + 1, :, pl.ds(1, 16), n * 4 + q, :],
                        out.at[n, :, x, :, pl.ds(q * 128, 128)], out_sem.at[x],
                    ).start()

    def chunk_in(i):
        t, s = ORDER[i]
        source_part(s * 4 + t)
        if i + LOOKAHEAD < CHUNKS:
            t, s = ORDER[i + LOOKAHEAD]
            raw_start(s * 4 + t)

    chunk_in(0)
    ghosts()
    for i, (t, s) in enumerate(ORDER):
        if i + 1 < CHUNKS:
            chunk_in(i + 1)
        source_rest(s * 4 + t)
        wave(t, s)
        for later in LATER.get((t, s), ()):
            wave(*later)
    for later in ENDING:
        wave(*later)
    first_sweep(0)
    wave(8, SLABS - 1)
    wave(9, SLABS - 1)
    first_sweep(1)
    coarse_halo(1)
    second_sweep(1)
    second_sweep(2)
    coarse_halo(0)
    second_sweep(0)
    second_sweep(3)

    for level in (4, 5):
        for s in range(SLABS):
            x_sent(level, s)
        for x in range(8):
            zface(level, x).wait_send()
    for q in range(CHUNKS):
        for x, first, second in planes(q):
            sums(q, x, second).wait_send()
    for r in (1, 2, 3):
        edge(r).wait_send()
    for kind in range(2):
        px_sent(kind)
        for group in range(2):
            pz(kind, group).wait_send()
    for x in range(8):
        view = S.at[x + 1, :, pl.ds(1, 16)]
        pltpu.make_async_copy(view, view, out_sem.at[x]).wait()


def leg(forcing, start, kappa, coupling, lag):
    f32 = jnp.float32
    vmem = pltpu.VMEM
    dma = pltpu.SemaphoreType.DMA
    hbm = pl.BlockSpec(memory_space=pltpu.HBM)
    smem = pl.BlockSpec(memory_space=pltpu.SMEM)
    block = (8, 5, 16, 8, 128)
    halo = (10, 5, 18, 8, 128)
    return pl.pallas_call(
        leg_kernel,
        out_shape=jax.ShapeDtypeStruct(start.shape, f32),
        in_specs=[hbm, hbm, hbm, smem, smem],
        out_specs=hbm,
        scratch_shapes=[
            vmem(halo, f32), vmem(halo, f32), vmem(halo, f32),
            vmem(block, f32), vmem(block, f32), vmem(block, f32), vmem(block, f32),
            vmem((8, 16, 8, 128), f32), vmem((8, 16, 8, 128), f32),
            vmem((5, 2, 8, 128), f32), vmem((3, 5, 2, 8, 128), f32), vmem((5, 2, 8, 128), f32),
            vmem((4, 5, 8, 8, 128), f32), vmem((4, 8, 8, 128), f32),
            vmem((6, 5, 10, 8, 128), f32),
            vmem((2, 2, 5, 4, 8, 128), f32), vmem((2, 2, 5, 4, 8, 128), f32),
            vmem((2, 2, 5, 8, 128), f32), vmem((2, 2, 5, 8, 128), f32),
            dma((8,)), dma((8,)), dma((1,)),
            dma((2 * CHUNKS,)), dma((2 * CHUNKS,)), dma((2 * CHUNKS,)), dma((2 * CHUNKS,)),
            dma((3,)), dma((3,)),
            dma((6 * SLABS,)), dma((6 * SLABS,)), dma((24,)), dma((24,)),
            dma((4,)), dma((4,)), dma((4,)), dma((4,)), dma((8,)),
        ],
        compiler_params=pltpu.CompilerParams(
            collective_id=0, has_side_effects=True, vmem_limit_bytes=56 * 2**20
        ),
        name="leg",
    )(forcing, start, kappa, coupling, lag)


def shards(forcing, state_start, kappa, coupling, lag):
    return leg(forcing, state_start, kappa, coupling, lag)


def solution(mesh):
    return jax.shard_map(
        shards,
        mesh=mesh,
        in_specs=(
            P("instance", None, "space", "coarse", None),
            P("instance", None, "space", "coarse", None),
            P("space", "coarse", None),
            P(),
            P("coarse"),
        ),
        out_specs=P("instance", None, "space", "coarse", None),
        check_vma=False,
    )
```

```python
import functools
import math

import jax
import jax.numpy as jnp
import numpy as np
from jax import lax
from jax.experimental import pallas as pl
from jax.experimental.pallas import tpu as pltpu
from jax.sharding import PartitionSpec as P

MESH = pl.DeviceIdType.MESH
WEIGHTS = (0.25, 0.5, 1.0)
STAGES = 6
CUTS = (0, 8, 12, 16)
SLABS = len(CUTS) - 1
CHUNKS = 4 * SLABS
ORDER = ((0, 0), (1, 0), (0, 1), (2, 0), (3, 0), (1, 1), (0, 2), (2, 1), (1, 2), (3, 1), (2, 2), (3, 2))
LATER = {(2, 1): ((4, 0),), (3, 1): ((5, 0),), (2, 2): ((4, 1), (6, 0)), (3, 2): ((5, 1), (7, 0))}
ENDING = ((4, 2), (6, 1), (8, 0), (9, 0), (5, 2), (7, 1), (6, 2), (8, 1), (9, 1), (7, 2))
LOOKAHEAD = 2
WIDE = 4


def spectral(d):
    if d == 0:
        return 0.0
    return float(0.5 * (-1.0) ** abs(d) * math.cos(math.pi * d / 8) / math.sin(math.pi * d / 8))


D1, D2, D3, D4 = spectral(1), spectral(2), spectral(3), spectral(4)


def leg_kernel(
    forcing, start, kappa, coupling, lag, out,
    S, A, B, F, R1, C2, R2, K, W, E, EG, GP, RHS, WC, E1, XO, XI, ZO, ZI, WI,
    ld_s, ld_f, ld_k, p1s, p1r, p2s, p2r, es, er, xs_s, xs_r, zs_s, zs_r, px_s, px_r, pz_s, pz_r, wc_s, wc_r, out_sem,
):
    comps = 5
    sp, it, co = lax.axis_index("space"), lax.axis_index("instance"), lax.axis_index("coarse")
    spaces = lax.axis_size("space")
    odd = lax.rem(it, 2)
    pa = lax.rem(it + 1 + 2 * odd, 4)
    pb = lax.rem(it + 3 + 2 * odd, 4)
    has_lo, has_hi = sp > 0, sp < spaces - 1

    sub = lax.broadcasted_iota(jnp.int32, (8, 128), 0)
    lane = lax.broadcasted_iota(jnp.int32, (8, 128), 1)
    inst = sub // 4
    quarter = sub % 4

    def zrange(d0, d1):
        return (1 - co) * (16 - d1) + co * d0

    def turn(v, shift, axis):
        if v.ndim == 2:
            return pltpu.roll(v, shift, axis)
        if axis == 1:
            return pltpu.roll(v.reshape(-1, 128), shift, 1).reshape(v.shape)
        return jnp.stack([pltpu.roll(v[i], shift, 0) for i in range(v.shape[0])])

    order = (0, 7, 1, 6, 2, 5, 3, 4)
    for x in order:
        for n in range(2):
            for q in range(4):
                pltpu.make_async_copy(
                    start.at[n, :, x, :, pl.ds(q * 128, 128)],
                    S.at[x + 1, :, pl.ds(1, 16), n * 4 + q, :], ld_s.at[x],
                ).start()
    for n in range(2):
        for q in range(4):
            pltpu.make_async_copy(
                kappa.at[:, :, pl.ds(q * 128, 128)], K.at[:, :, n * 4 + q, :], ld_k.at[0]
            ).start()
    for x in order:
        for n in range(2):
            for q in range(4):
                pltpu.make_async_copy(
                    forcing.at[n, :, x, :, pl.ds(q * 128, 128)],
                    F.at[x, :, :, n * 4 + q, :], ld_f.at[x],
                ).start()

    zero16 = jnp.zeros((comps, 16, 8, 128), jnp.float32)
    zero1 = jnp.zeros((comps, 8, 128), jnp.float32)
    zero4 = jnp.zeros((comps, 4, 8, 128), jnp.float32)
    zero8 = jnp.zeros((comps, 8, 8, 128), jnp.float32)
    zend = 17 * co
    zend_c = 9 * co

    for x in range(8):
        for buf in (S, A, B):
            buf[x + 1, :, zend] = zero1
    for x in range(4):
        E1[x + 1, :, zend_c] = zero1

    @pl.when(sp == 0)
    def _():
        for buf in (S, A, B):
            buf[0, :, pl.ds(1, 16)] = zero16
        E1[0, :, pl.ds(1, 8)] = zero8
        XI[0, 1] = zero4

    @pl.when(sp == spaces - 1)
    def _():
        for buf in (S, A, B):
            buf[9, :, pl.ds(1, 16)] = zero16
        E1[5, :, pl.ds(1, 8)] = zero8
        XI[0, 0] = zero4

    bar = pltpu.get_barrier_semaphore()
    for r in (1, 2, 3):
        pl.semaphore_signal(bar, inc=1, device_id={"instance": lax.rem(it + r, 4)}, device_id_type=MESH)
    pl.semaphore_signal(bar, inc=1, device_id={"coarse": 1 - co}, device_id_type=MESH)

    @pl.when(has_lo)
    def _():
        pl.semaphore_signal(bar, inc=1, device_id={"space": sp - 1}, device_id_type=MESH)

    @pl.when(has_hi)
    def _():
        pl.semaphore_signal(bar, inc=1, device_id={"space": sp + 1}, device_id_type=MESH)

    pl.semaphore_wait(bar, 4 + has_lo.astype(jnp.int32) + has_hi.astype(jnp.int32))

    def level_range(level, s):
        back = max(level - 1, 0)
        return (CUTS[s] - back if s > 0 else 0, CUTS[s + 1] - back if s < SLABS - 1 else 16)

    def level_buf(level):
        return (S, A, B)[level % 3]

    def xface(level, s, side):
        d0, d1 = level_range(level, s)
        z0 = 1 + zrange(d0, d1)
        buf = level_buf(level)
        i = ((level % 3) * SLABS + s) * 2 + side
        return pltpu.make_async_remote_copy(
            buf.at[1 if side == 0 else 8, :, pl.ds(z0, d1 - d0)],
            buf.at[9 if side == 0 else 0, :, pl.ds(z0, d1 - d0)],
            xs_s.at[i], xs_r.at[i],
            device_id={"space": sp - 1 if side == 0 else sp + 1}, device_id_type=MESH,
        )

    def x_send(level, s):
        pl.when(has_lo)(lambda: xface(level, s, 0).start())
        pl.when(has_hi)(lambda: xface(level, s, 1).start())

    def x_sent(level, s):
        pl.when(has_lo)(lambda: xface(level, s, 0).wait_send())
        pl.when(has_hi)(lambda: xface(level, s, 1).wait_send())

    def x_recv(level, s):
        pl.when(has_hi)(lambda: xface(level, s, 0).wait_recv())
        pl.when(has_lo)(lambda: xface(level, s, 1).wait_recv())

    def zface(level, x):
        buf = level_buf(level)
        i = (level % 3) * 8 + x
        return pltpu.make_async_remote_copy(
            buf.at[x + 1, :, pl.ds(16 - 15 * co, 1)], buf.at[x + 1, :, pl.ds(17 * co, 1)],
            zs_s.at[i], zs_r.at[i], device_id={"coarse": 1 - co}, device_id_type=MESH,
        )

    def planes(q):
        t = q % 4
        return ((t, pa, pb), (7 - t, pb, pa))

    def chunk(q):
        d0, d1 = CUTS[q // 4], CUTS[q // 4 + 1]
        return zrange(d0, d1), d1 - d0

    def raw(q, x, partner):
        z0, n = chunk(q)
        i = q * 2 + (0 if x < 4 else 1)
        return pltpu.make_async_remote_copy(
            S.at[x + 1, :, pl.ds(1 + z0, n)], R1.at[x, :, pl.ds(z0, n)],
            p1s.at[i], p1r.at[i], device_id={"instance": partner}, device_id_type=MESH,
        )

    def sums(q, x, partner):
        z0, n = chunk(q)
        i = q * 2 + (0 if x < 4 else 1)
        return pltpu.make_async_remote_copy(
            C2.at[x, :, pl.ds(z0, n)], R2.at[x, :, pl.ds(z0, n)],
            p2s.at[i], p2r.at[i], device_id={"instance": partner}, device_id_type=MESH,
        )

    def raw_start(q):
        for x, first, second in planes(q):
            raw(q, x, first).start()

    for x in order:
        view = S.at[x + 1, :, pl.ds(1, 16)]
        pltpu.make_async_copy(view, view, ld_s.at[x]).wait()
        for t, s in ORDER[:LOOKAHEAD]:
            if t == 7 - x:
                raw_start(s * 4 + t)
    for s in range(SLABS):
        x_send(0, s)
    for x in order:
        zface(0, x).start()

    def pack(z, carry):
        for c in range(comps):
            for xh in range(2):
                total = E[c, xh]
                for xq in range(4):
                    v = pltpu.roll(S[xh * 4 + xq + 1, c, z + 1], xq * 32 + 2 * z + 1, 1)
                    total = jnp.where((lane // 2) == xq * 16 + z, v, total)
                E[c, xh] = total
        return carry

    E[...] = jnp.zeros_like(E)
    lax.fori_loop(0, 16, pack, 0)

    def edge(r):
        return pltpu.make_async_remote_copy(
            E, EG.at[r - 1], es.at[r - 1], er.at[r - 1],
            device_id={"instance": lax.rem(it + r, 4)}, device_id_type=MESH,
        )

    for r in (1, 2, 3):
        edge(r).start()

    pltpu.make_async_copy(K, K, ld_k.at[0]).wait()
    even_lane = lane % 2 == 0

    def pair_sum(v):
        return v + jnp.where(even_lane, turn(v, 127, 1), turn(v, 1, 1))

    def steps(i, carry):
        z = i * 4
        for xc in range(4):
            k0, k1 = K[2 * xc, pl.ds(z, 4)], K[2 * xc + 1, pl.ds(z, 4)]
            W[2 * xc, pl.ds(z, 4)] = 0.8 / (6.0 + k0)
            W[2 * xc + 1, pl.ds(z, 4)] = 0.8 / (6.0 + k1)
            total = (k0 + k1).reshape(2, 2, 8, 128)
            WC[xc, pl.ds(2 * i, 2)] = 0.8 / (6.0 + pair_sum(total[:, 0] + total[:, 1]) * 0.125)
        return carry

    lax.fori_loop(0, 4, steps, 0)

    def wc(side):
        return pltpu.make_async_remote_copy(
            WC.at[0 if side == 0 else 3], WI.at[side], wc_s.at[side], wc_r.at[side],
            device_id={"space": sp - 1 if side == 0 else sp + 1}, device_id_type=MESH,
        )

    pl.when(has_lo)(lambda: wc(0).start())
    pl.when(has_hi)(lambda: wc(1).start())

    for x in order:
        view = F.at[x]
        pltpu.make_async_copy(view, view, ld_f.at[x]).wait()

    def ghosts():
        zl = (lane % 32) // 2
        lags = jnp.zeros((8, 128), jnp.int32)
        for z in range(16):
            lags = jnp.where(zl == z, lag[z], lags)
        mine = 2 * it + inst
        low = (mine - lags + 8) % 8
        high = (mine + lags) % 8
        want = jnp.where(
            (quarter == 0) & (lane % 2 == 1), low, jnp.where((quarter == 3) & (lane % 2 == 0), high, -1)
        )
        low_slot = lane % 2 == 1
        for r in (1, 2, 3):
            edge(r).wait_recv()
        for c in range(comps):
            for xh in range(2):
                total = jnp.zeros((8, 128), jnp.float32)
                for r in range(4):
                    p = E[c, xh] if r == 0 else EG[r - 1, c, xh]
                    who = lax.rem(it + 4 - r, 4)
                    up, down = pltpu.roll(p, 1, 1), pltpu.roll(p, 127, 1)
                    same = jnp.where(low_slot, pltpu.roll(up, 5, 0), pltpu.roll(down, 3, 0))
                    other = jnp.where(low_slot, pltpu.roll(up, 1, 0), pltpu.roll(down, 7, 0))
                    total = jnp.where(want == 2 * who + inst, same, total)
                    total = jnp.where(want == 2 * who + 1 - inst, other, total)
                GP[c, xh] = total

        ends = ((lane == 0) & (quarter == 0)) | ((lane == 127) & (quarter == 3))

        def unpack(z, carry):
            for xh in range(2):
                for c in range(comps):
                    g = GP[c, xh]
                    for xq in range(4):
                        x = xh * 4 + xq
                        v = pltpu.roll(g, 127 - xq * 32 - 2 * z, 1)
                        F[x, c, z] = F[x, c, z] + jnp.where(ends, v, 0.0)
            return carry

        lax.fori_loop(0, 16, unpack, 0)

    def by_inst(v0, v1):
        return jnp.where(inst == 0, v0, v1).astype(jnp.float32)

    delta = by_inst(-D1, D1)
    gamma = by_inst(D3, -D3)
    plus = by_inst(D1, D3)
    minus = by_inst(-D3, -D1)

    def source_part(q):
        z0, n = chunk(q)
        for x, first, second in planes(q):
            raw(q, x, first).wait_recv()
        for x, first, second in planes(q):
            up = odd == (1 if x < 4 else 0)
            alpha = jnp.where(up, D2, -D2).astype(jnp.float32)
            beta = jnp.where(up, plus, minus)

            def part(i, carry):
                z = z0 + i * WIDE
                for c in range(comps):
                    u, v = S[x + 1, c, pl.ds(z + 1, WIDE)], R1[x, c, pl.ds(z, WIDE)]
                    ur, vr = turn(u, 4, 0), turn(v, 4, 0)
                    C2[x, c, pl.ds(z, WIDE)] = (alpha * u + beta * ur) + (D4 * v + gamma * vr)
                    F[x, c, pl.ds(z, WIDE)] = F[x, c, pl.ds(z, WIDE)] - (delta * ur + (alpha * v + beta * vr))
                return carry

            lax.fori_loop(0, n // WIDE, part, 0)
            sums(q, x, second).start()

    def source_rest(q):
        z0, n = chunk(q)
        for x, first, second in planes(q):
            sums(q, x, second).wait_recv()
            raw(q, x, first).wait_send()

        def rest(i, carry):
            z = pl.ds(z0 + i * WIDE, WIDE)
            for x, first, second in planes(q):
                for c in range(comps):
                    F[x, c, z] = F[x, c, z] - R2[x, c, z]
            return carry

        lax.fori_loop(0, n // WIDE, rest, 0)

    lane_lo, lane_hi = lane == 0, lane == 127
    fix_lo = lane_lo & (quarter != 0)
    fix_hi = lane_hi & (quarter != 3)

    def pick(mask, a, b):
        return jnp.where(jnp.broadcast_to(mask, a.shape), a, b)

    def beside_y(u):
        lo, hi = turn(u, 1, 1), turn(u, 127, 1)
        zero = jnp.zeros_like(u)
        lower = pick(fix_lo, turn(lo, 1, 0), pick(lane_lo, zero, lo))
        upper = pick(fix_hi, turn(hi, 7, 0), pick(lane_hi, zero, hi))
        return lower + upper

    def mix(us, c):
        total = coupling[c, 0] * us[0]
        for d in range(1, comps):
            total = total + coupling[c, d] * us[d]
        return total

    def balance(buf, x, z, n):
        us = [buf[x + 1, c, pl.ds(z + 1, n)] for c in range(comps)]
        ys = [beside_y(u) for u in us]
        got = []
        for c in range(comps):
            near = (buf[x, c, pl.ds(z + 1, n)] + buf[x + 2, c, pl.ds(z + 1, n)]) + (
                buf[x + 1, c, pl.ds(z, n)] + buf[x + 1, c, pl.ds(z + 2, n)]
            )
            got.append((F[x, c, pl.ds(z, n)] + near) + (ys[c] - mix(us, c)))
        return us, got

    def stage_cells(k, j, z, n):
        src, dst, weight = level_buf(k - 1), level_buf(k), WEIGHTS[(k - 1) % 3]
        for x in (j, 7 - j):
            us, got = balance(src, x, z, n)
            w = W[x, pl.ds(z, n)] * weight
            for c in range(comps):
                own = us[c] if src is S else S[x + 1, c, pl.ds(z + 1, n)]
                dst[x + 1, c, pl.ds(z + 1, n)] = (own - (0.8 * weight) * us[c]) + w * got[c]

    def last_cells(j, z, n):
        half = z // 2
        for x in (j, 7 - j):
            us, got = balance(S, x, z, n)
            diag = 6.0 + K[x, pl.ds(z, n)]
            for c in range(comps):
                res = (got[c] - diag * us[c]).reshape(n // 2, 2, 8, 128)
                total = res[:, 0] + res[:, 1]
                if j % 2 == 1:
                    total = total + RHS[x // 2, c, pl.ds(half, n // 2)]
                RHS[x // 2, c, pl.ds(half, n // 2)] = total

    def run(k, j, s):
        if j == 0 and k <= STAGES:
            x_recv(k - 1, s)
            if k >= 3:
                x_sent(k - 3, s)
        if s == 0 and k <= STAGES:
            for x in (j, 7 - j):
                zface(k - 1, x).wait_recv()
                if k >= 3:
                    zface(k - 3, x).wait_send()
        d0, d1 = level_range(k, s)
        z0, n = zrange(d0, d1), d1 - d0
        cells = functools.partial(stage_cells, k) if k <= STAGES else last_cells
        wide, rest = divmod(n, WIDE)

        def many(i, carry):
            cells(j, z0 + i * WIDE, WIDE)
            return carry

        if wide:
            lax.fori_loop(0, wide, many, 0)
        if rest:
            cells(j, z0 + wide * WIDE, rest)
        if k < STAGES:
            if j == 0:
                x_send(k, s)
            if s == 0:
                for x in (j, 7 - j):
                    zface(k, x).start()
        if k == 4:
            if j == 0:
                for x in (0, 9):
                    S[x, :, pl.ds(1 + z0, n)] = jnp.zeros((comps, n, 8, 128), jnp.float32)
            if s == 0:
                for x in (j, 7 - j):
                    S[x + 1, :, 17 * (1 - co)] = zero1
        if k == STAGES:
            if j == 0 and s == SLABS - 1:
                smooth_x()
            if j % 2 == 1 and s == 0:
                smooth_z(j // 2)

    def wave(t, s):
        for k in range(max(1, t - 2), min(STAGES + 1, t + 1) + 1):
            run(k, t + 1 - k, s)

    def px(kind, side):
        return pltpu.make_async_remote_copy(
            XO.at[kind, side], XI.at[kind, side], px_s.at[kind * 2 + side], px_r.at[kind * 2 + side],
            device_id={"space": sp - 1 if side == 0 else sp + 1}, device_id_type=MESH,
        )

    def px_start(kind):
        pl.when(has_lo)(lambda: px(kind, 0).start())
        pl.when(has_hi)(lambda: px(kind, 1).start())

    def px_sent(kind):
        pl.when(has_lo)(lambda: px(kind, 0).wait_send())
        pl.when(has_hi)(lambda: px(kind, 1).wait_send())

    def px_recv(kind):
        pl.when(has_hi)(lambda: px(kind, 0).wait_recv())
        pl.when(has_lo)(lambda: px(kind, 1).wait_recv())

    def pz(kind, group):
        i = kind * 2 + group
        return pltpu.make_async_remote_copy(
            ZO.at[kind, group], ZI.at[kind, group], pz_s.at[i], pz_r.at[i],
            device_id={"coarse": 1 - co}, device_id_type=MESH,
        )

    def join(first, second):
        return pick(even_lane, first + turn(first, 127, 1), second + turn(second, 1, 1))

    def smooth_x():
        for side, x in ((0, 1), (1, 8)):
            for c in range(comps):
                v = S[x, c, pl.ds(1, 16)].reshape(4, 2, 2, 8, 128)
                v = v[:, :, 0] + v[:, :, 1]
                XO[0, side, c] = join(v[:, 0], v[:, 1])
        px_start(0)

    def smooth_z(group):
        zi = 16 - 15 * co
        for c in range(comps):
            v = [S[2 * xc + 1, c, zi] + S[2 * xc + 2, c, zi] for xc in (group, 3 - group)]
            ZO[0, group, c] = join(v[0], v[1])
        pz(0, group).start()

    zc_in = 7 * (1 - co)

    def spread(v):
        parts = [pick(even_lane, v, turn(v, 1, 1)), pick(even_lane, turn(v, 127, 1), v)]
        return jnp.stack(parts, 1).reshape(8, 8, 128)

    def first_sweep(group):
        pz(0, group).wait_recv()
        for i, xc in enumerate((group, 3 - group)):
            mask = even_lane if i == 0 else ~even_lane
            for c in range(comps):
                RHS[xc, c, zc_in] = RHS[xc, c, zc_in] + jnp.where(mask, ZI[0, group, c], 0.0)
        for xc in (group, 3 - group):
            for c in range(comps):
                E1[xc + 1, c, pl.ds(1, 8)] = WC[xc] * pair_sum(RHS[xc, c])

    def share_x():
        for side, xc in ((0, 0), (1, 3)):
            for c in range(comps):
                v = E1[xc + 1, c, pl.ds(1, 8)].reshape(4, 2, 8, 128)
                XO[1, side, c] = pick(even_lane, v[:, 0], v[:, 1])
        px_start(1)

    def finish_x():
        px_recv(0)
        for side, xc in ((1, 0), (0, 3)):
            for c in range(comps):
                E1[xc + 1, c, pl.ds(1, 8)] = E1[xc + 1, c, pl.ds(1, 8)] + WC[xc] * spread(XI[0, side, c])

    def share_z(group):
        for c in range(comps):
            ZO[1, group, c] = jnp.where(even_lane, E1[group + 1, c, 1 + zc_in], E1[4 - group, c, 1 + zc_in])
        pz(1, group).start()

    def coarse_halo(group):
        pz(1, group).wait_recv()
        for c in range(comps):
            v = ZI[1, group, c]
            E1[group + 1, c, 9 * (1 - co)] = jnp.where(even_lane, v, pltpu.roll(v, 1, 1))
            E1[4 - group, c, 9 * (1 - co)] = jnp.where(even_lane, pltpu.roll(v, 127, 1), v)
        if group == 0:

            def unpack(side, x):
                for c in range(comps):
                    E1[x, c, pl.ds(1, 8)] = spread(XI[1, side, c]) + WI[side] * spread(XO[0, 1 - side, c])

            @pl.when(has_hi)
            def _():
                wc(0).wait_recv()
                px(1, 0).wait_recv()
                unpack(0, 5)

            @pl.when(has_lo)
            def _():
                wc(1).wait_recv()
                px(1, 1).wait_recv()
                unpack(1, 0)

    lo2, hi2 = lane < 2, lane >= 126
    first_q, last_q = quarter == 0, quarter == 3

    def beside_y2(u):
        lo, hi = turn(u, 2, 1), turn(u, 126, 1)
        wrap_lo = pick(first_q, turn(lo, 5, 0), turn(lo, 1, 0))
        wrap_hi = pick(last_q, turn(hi, 3, 0), turn(hi, 7, 0))
        return pick(lo2, wrap_lo, lo) + pick(hi2, wrap_hi, hi)

    def second_sweep(xc):
        def body(i, carry):
            z = i * 4
            mid = pl.ds(z + 1, 4)
            ee = [E1[xc + 1, c, mid] for c in range(comps)]
            w = WC[xc, pl.ds(z, 4)]
            for c in range(comps):
                near = (E1[xc, c, mid] + E1[xc + 2, c, mid]) + (
                    E1[xc + 1, c, pl.ds(z, 4)] + E1[xc + 1, c, pl.ds(z + 2, 4)]
                )
                e = 1.2 * ee[c] + w * ((near + beside_y2(ee[c])) - mix(ee, c))
                fine = jnp.broadcast_to(e[:, None], (4, 2, 8, 128)).reshape(8, 8, 128)
                for x in (2 * xc, 2 * xc + 1):
                    at = pl.ds(2 * z + 1, 8)
                    S[x + 1, c, at] = S[x + 1, c, at] + fine
            return carry

        lax.fori_loop(0, 2, body, 0)
        for x in (2 * xc, 2 * xc + 1):
            for n in range(2):
                for q in range(4):
                    pltpu.make_async_copy(
                        S.at[x + 1, :, pl.ds(1, 16), n * 4 + q, :],
                        out.at[n, :, x, :, pl.ds(q * 128, 128)], out_sem.at[x],
                    ).start()

    def chunk_in(i):
        t, s = ORDER[i]
        source_part(s * 4 + t)
        if i + LOOKAHEAD < CHUNKS:
            t, s = ORDER[i + LOOKAHEAD]
            raw_start(s * 4 + t)

    chunk_in(0)
    ghosts()
    for i, (t, s) in enumerate(ORDER):
        if i + 1 < CHUNKS:
            chunk_in(i + 1)
        source_rest(s * 4 + t)
        wave(t, s)
        for later in LATER.get((t, s), ()):
            wave(*later)
    for later in ENDING:
        wave(*later)
    first_sweep(0)
    share_x()
    wave(8, SLABS - 1)
    wave(9, SLABS - 1)
    first_sweep(1)
    share_z(1)
    finish_x()
    share_z(0)
    coarse_halo(1)
    second_sweep(1)
    second_sweep(2)
    coarse_halo(0)
    second_sweep(0)
    second_sweep(3)

    for level in (4, 5):
        for s in range(SLABS):
            x_sent(level, s)
        for x in range(8):
            zface(level, x).wait_send()
    for q in range(CHUNKS):
        for x, first, second in planes(q):
            sums(q, x, second).wait_send()
    for r in (1, 2, 3):
        edge(r).wait_send()
    pl.when(has_lo)(lambda: wc(0).wait_send())
    pl.when(has_hi)(lambda: wc(1).wait_send())
    for kind in range(2):
        px_sent(kind)
        for group in range(2):
            pz(kind, group).wait_send()
    for x in range(8):
        view = S.at[x + 1, :, pl.ds(1, 16)]
        pltpu.make_async_copy(view, view, out_sem.at[x]).wait()


def leg(forcing, start, kappa, coupling, lag):
    f32 = jnp.float32
    vmem = pltpu.VMEM
    dma = pltpu.SemaphoreType.DMA
    hbm = pl.BlockSpec(memory_space=pltpu.HBM)
    smem = pl.BlockSpec(memory_space=pltpu.SMEM)
    block = (8, 5, 16, 8, 128)
    halo = (10, 5, 18, 8, 128)
    return pl.pallas_call(
        leg_kernel,
        out_shape=jax.ShapeDtypeStruct(start.shape, f32),
        in_specs=[hbm, hbm, hbm, smem, smem],
        out_specs=hbm,
        scratch_shapes=[
            vmem(halo, f32), vmem(halo, f32), vmem(halo, f32),
            vmem(block, f32), vmem(block, f32), vmem(block, f32), vmem(block, f32),
            vmem((8, 16, 8, 128), f32), vmem((8, 16, 8, 128), f32),
            vmem((5, 2, 8, 128), f32), vmem((3, 5, 2, 8, 128), f32), vmem((5, 2, 8, 128), f32),
            vmem((4, 5, 8, 8, 128), f32), vmem((4, 8, 8, 128), f32),
            vmem((6, 5, 10, 8, 128), f32),
            vmem((2, 2, 5, 4, 8, 128), f32), vmem((2, 2, 5, 4, 8, 128), f32),
            vmem((2, 2, 5, 8, 128), f32), vmem((2, 2, 5, 8, 128), f32),
            vmem((2, 8, 8, 128), f32),
            dma((8,)), dma((8,)), dma((1,)),
            dma((2 * CHUNKS,)), dma((2 * CHUNKS,)), dma((2 * CHUNKS,)), dma((2 * CHUNKS,)),
            dma((3,)), dma((3,)),
            dma((6 * SLABS,)), dma((6 * SLABS,)), dma((24,)), dma((24,)),
            dma((4,)), dma((4,)), dma((4,)), dma((4,)), dma((2,)), dma((2,)), dma((8,)),
        ],
        compiler_params=pltpu.CompilerParams(
            collective_id=0, has_side_effects=True, vmem_limit_bytes=56 * 2**20
        ),
        name="leg",
    )(forcing, start, kappa, coupling, lag)


def shards(forcing, state_start, kappa, coupling, lag):
    return leg(forcing, state_start, kappa, coupling, lag)


def solution(mesh):
    return jax.shard_map(
        shards,
        mesh=mesh,
        in_specs=(
            P("instance", None, "space", "coarse", None),
            P("instance", None, "space", "coarse", None),
            P("space", "coarse", None),
            P(),
            P("coarse"),
        ),
        out_specs=P("instance", None, "space", "coarse", None),
        check_vma=False,
    )
```
